256 devices in a mesh: section: 2 (over core), expert: 128 (over y, x, z).
Axes of the slice: x: 4, y: 4, z: 8, core: 2. Of those that a mesh axis runs over, the one named last changes fastest.
Arguments:
- source_tokens: bfloat16 [32768, 2048], P(('section', 'expert')), may hold values from -6 to 6
- routes: int32 [32768, 2], P(('section', 'expert')), may hold values from 0 to 63, all different within a row; in each aligned block of 128 rows (0 to 127, 128 to 255, ...) at most 5 rows name the same one
- gates: float32 [32768, 2], P(('section', 'expert')), may hold values from 0.1 to 1
- source_sentence: int32 [256, 128], P(('section', 'expert')), may hold values from 0 to 3, never falling along the last dimension, each value on 1 to 64 neighbouring positions
- expert_in: bfloat16 [128, 2048, 2048], P('expert', None, 'section'), may hold values from -0.125 to 0.125
- expert_out: bfloat16 [128, 2048, 2048], P('expert', 'section'), may hold values from -0.09375 to 0.09375
- final_gain: float32 [2048], replicated, may hold values from 0.1 to 1.9
- target_tokens: bfloat16 [65536, 2048], P(('section', 'expert')), may hold values from -256 to 256
- target_sentence: int32 [256, 256], P(('section', 'expert')), may hold values from 0 to 3, never falling along the last dimension, each value on 1 to 128 neighbouring positions
- query_weight: bfloat16 [2048, 1024], P(('section', 'expert')), may hold values from -0.125 to 0.125
- key_weight: bfloat16 [2048, 1024], P(('section', 'expert')), may hold values from -0.125 to 0.125
- value_weight: bfloat16 [2048, 1024], P(('section', 'expert')), may hold values from -0.125 to 0.125
Outputs:
- memory: bfloat16 [32768, 2048], P(('section', 'expert'))
- context: bfloat16 [65536, 1024], P(('section', 'expert'))
The draws below stay inside these ranges and needn't reach their ends.
Inputs may be any that keep to these rules, and one draw needn't show every extreme that they name: `routes`: each row names two different experts; among the 128 rows of one device no expert is named more than 5 times, a bound that some block reaches. `source_sentence`: within a block the numbers never fall and all 4 sentences appear. `target_sentence`: within a block the numbers never fall and all 4 sentences appear.
All inputs are finite; a program needn't handle non-finite values.
Results may differ from the reference program's by a relative error of at most 0.035.
Values may be sent and summed in bfloat16 or wider, within the bound.
A program may use at most 128 MiB of HBM per device.

```python
import math
import jax
import jax.numpy as jnp
import numpy as np
from jax import lax

D = 2048
FFW = 4096
HEADS = 8
HDIM = 128
SENTS = 4
TOK_DEV = 128
TGT_DEV = 256
EXPERTS = 64
CAP = 5
HD = 1024
SRC_TOKENS = 32768
TGT_TOKENS = 65536
N_EXPERT = 128
DEVICES = 256


def draw_target_tokens(key, part):
    key = jax.random.fold_in(key, 11)
    first = jax.random.fold_in(key, 0)
    base = jax.random.normal(first, (TGT_TOKENS, D), jnp.float32)
    return base.astype(jnp.bfloat16)


def level_of(own_key, dims, shards, low, top_value):
    level, own = 1.0, jax.random.fold_in(own_key, 6)
    for position, shards_of in shards:
        heights = jnp.exp(jax.random.uniform(jax.random.fold_in(own, position), (shards_of,), jnp.float32, low / len(shards), top_value / len(shards)))
        level = level * jnp.repeat(heights, dims[position] // shards_of).reshape([-1 if axis == position else 1 for axis in range(len(dims))])
    return level


def length_profile(amount, total, limit, skew):
    loads = [(1 << 20) // math.isqrt(standing ** skew) + 1 for standing in range(2, amount + 1)]
    surplus, holding = total - limit - (amount - 1), [1] * (amount - 1)
    while surplus > 0:
        candidates = [i for i in range(amount - 1) if holding[i] < limit]
        whole, budget = sum([loads[i] for i in candidates]), surplus
        for i in candidates:
            addition = min(limit - holding[i], max(1, budget * loads[i] // whole), surplus)
            holding[i] = holding[i] + addition
            surplus = surplus - addition
    return np.array([limit] + holding)


def ragged_sizes(own_key, amount, total, most, slope):
    if amount == 2:
        one = jax.random.randint(own_key, (), max(1, total - most), min(most, total - 1) + 1)
        return jnp.stack([one, total - one])
    lengths = jnp.asarray(length_profile(amount, total, most, slope), jnp.int32)
    pairs = (amount - 1) // 2
    giver, sink = lengths[1:1 + 2 * pairs:2], lengths[2:2 + 2 * pairs:2]
    margin = jnp.minimum(giver - 1, most - sink)
    passed = jax.random.randint(jax.random.fold_in(own_key, 1), (pairs,), 0, 1 << 20) % (margin + 1)
    lengths = lengths.at[1:1 + 2 * pairs:2].set(giver - passed).at[2:2 + 2 * pairs:2].set(sink + passed)
    return lengths[jax.random.permutation(jax.random.fold_in(own_key, 2), amount)]


def assign_block(own_key, own, number, rows, amount, top, most, slope):
    sequence = jax.random.permutation(own_key, amount)
    heavy_load, usual = portions_of(amount, rows * top, most, slope, True), portions_of(amount, rows * top, most, slope, False)
    places = jnp.arange(amount)

    def named(tallies, rotation):
        used = int((tallies > 0).sum())
        fixed = max(1, used // 4)
        moved = fixed + (places - fixed + rotation * (used - fixed)) % max(1, amount - fixed)
        return jnp.zeros((amount,), jnp.int32).at[sequence[jnp.where(places < fixed, places, moved)]].set(jnp.asarray(tallies, jnp.int32))

    tallies = jnp.where(number % 4 == 0, named(heavy_load, number // 4), named(usual, number - number // 4 - 1))
    mixed = jax.random.permutation(jax.random.fold_in(own, 3), amount)
    donor, taker = mixed[0:amount // 2 * 2:2], mixed[1:amount // 2 * 2:2]
    slack = jnp.minimum(tallies[donor] - 1, most - tallies[taker]) // 2
    slack = jnp.where((donor == sequence[0]) | (taker == sequence[0]) | (tallies[taker] == 0), 0, jnp.maximum(slack, 0))
    moved = jax.random.randint(jax.random.fold_in(own, 4), (amount // 2,), 0, 1 << 20) % (slack + 1)
    tallies = tallies.at[donor].add(-moved).at[taker].add(moved)
    items = jnp.searchsorted(jnp.cumsum(tallies), jnp.arange(rows * top), side="right").astype(jnp.int32)
    table = items.reshape(top, rows).T
    table = table[jax.random.permutation(jax.random.fold_in(own, 1), rows)]
    rotation = jax.random.randint(jax.random.fold_in(own, 2), (rows, 1), 0, top)
    return jnp.take_along_axis(table, (jnp.arange(top)[None, :] + rotation) % top, axis=1)


def portions_of(count, total, most, skew, full):
    loads = [(1 << 20) // math.isqrt(rank ** skew) + 1 for rank in range(1, count + 1)]
    largest = most if full else min(most, max(-(-total // count), total * loads[0] // sum(loads)))
    least = 1 if total - largest >= count - 1 else 0
    given, rest = [largest] + [least] * (count - 1), total - largest - least * (count - 1)
    while rest > 0:
        movable = [i for i in range(1, count) if given[i] < largest] or [i for i in range(1, count) if given[i] < most]
        whole, budget = sum([loads[i] for i in movable]), rest
        for i in movable:
            more = min(most - given[i], max(1, budget * loads[i] // whole), rest)
            given[i] = given[i] + more
            rest = rest - more
    return np.array(given)


def normal_values(stream_key, extent, scale, bound, pieces=(), kind=jnp.bfloat16):
    entries = jax.random.normal(stream_key, extent, jnp.float32) * scale
    if len(pieces) > 0:
        entries = level_of(stream_key, extent, pieces, -0.22, 0.18) * entries
    return jnp.clip(entries, min=-bound, max=bound).astype(kind)


def setup_inputs(seed: int = 0) -> dict:
    seeds = jax.random.split(jax.random.key(seed), 13)
    source_tokens = normal_values(seeds[0], (SRC_TOKENS, D), 1.0, 6.0, ((0, 256),))
    routes_keys = jax.random.split(jax.random.fold_in(seeds[1], 1), SRC_TOKENS // TOK_DEV)
    routes_turns = jax.random.permutation(jax.random.fold_in(seeds[1], 3), SRC_TOKENS // TOK_DEV)
    routes = jax.vmap(lambda own, number: assign_block(jax.random.fold_in(seeds[1], 2), own, number, TOK_DEV, EXPERTS, 2, CAP, 2))(routes_keys, routes_turns).reshape((SRC_TOKENS, 2))
    gates = jnp.clip(0.1 + 0.9 * jax.random.uniform(seeds[2], (SRC_TOKENS, 2), jnp.float32) ** level_of(seeds[2], (SRC_TOKENS, 2), ((0, 256),), -0.2, 0.2), 0.1, 1.0)
    source_sentence = jax.vmap(lambda own: jnp.searchsorted(jnp.cumsum(ragged_sizes(own, SENTS, TOK_DEV, TOK_DEV // 2, 0)), jnp.arange(TOK_DEV), side="right"))(jax.random.split(seeds[3], DEVICES)).reshape((DEVICES, TOK_DEV)).astype(jnp.int32)
    expert_in = normal_values(seeds[4], (N_EXPERT, D, FFW // 2), D ** -0.5, 0.125, ((0, 128), (2, 2)))
    expert_out = normal_values(seeds[5], (N_EXPERT, FFW // 2, D), FFW ** -0.5, 0.09375, ((0, 128), (1, 2)))
    final_gain = jnp.clip(1.0 + 0.18 * jax.random.normal(seeds[6], (D,), jnp.float32), 0.1, 1.9)
    target_tokens = draw_target_tokens(jax.random.fold_in(seeds[12], 71), 0)
    target_sentence = jax.vmap(lambda own: jnp.searchsorted(jnp.cumsum(ragged_sizes(own, SENTS, TGT_DEV, TGT_DEV // 2, 0)), jnp.arange(TGT_DEV), side="right"))(jax.random.split(seeds[8], DEVICES)).reshape((DEVICES, TGT_DEV)).astype(jnp.int32)
    query_weight = normal_values(seeds[9], (D, HD), D ** -0.5, 0.125, ((0, 256),))
    key_weight = normal_values(seeds[10], (D, HD), D ** -0.5, 0.125, ((0, 256),))
    value_weight = normal_values(seeds[11], (D, HD), D ** -0.5, 0.125, ((0, 256),))
    return {"source_tokens": source_tokens, "routes": routes, "gates": gates, "source_sentence": source_sentence, "expert_in": expert_in, "expert_out": expert_out, "final_gain": final_gain, "target_tokens": target_tokens, "target_sentence": target_sentence, "query_weight": query_weight, "key_weight": key_weight, "value_weight": value_weight}


def layer_norm(values):
    mean = lax.optimization_barrier(jnp.mean(values, axis=-1, keepdims=True))
    centred = values - mean
    spread = lax.optimization_barrier(jnp.mean(centred * centred, axis=-1, keepdims=True))
    return centred * lax.rsqrt(spread + 1e-05)

def reference(source_tokens, routes, gates, source_sentence, expert_in, expert_out, final_gain, target_tokens, target_sentence, query_weight, key_weight, value_weight):
    total_rows = source_tokens.shape[0]
    normed = layer_norm(source_tokens.astype(jnp.float32)).astype(jnp.bfloat16)
    flat = routes.reshape(-1)
    total_pairs = flat.shape[0]
    picks = (flat[:, None] == jnp.arange(EXPERTS, dtype=jnp.int32)[None, :]).astype(jnp.int32)
    places = lax.optimization_barrier(jnp.sum((jnp.cumsum(picks, axis=0) - 1) * picks, axis=1)).astype(jnp.int32)
    slot_count = DEVICES * CAP
    slot_token = jnp.zeros((EXPERTS, slot_count), jnp.int32).at[flat, places].set(jnp.arange(total_pairs, dtype=jnp.int32) // 2)
    slot_gate = jnp.zeros((EXPERTS, slot_count), jnp.float32).at[flat, places].set(gates.reshape(-1))
    halves_in = expert_in.reshape(EXPERTS, 2, D, FFW // 2)
    halves_out = expert_out.reshape(EXPERTS, 2, FFW // 2, D)

    def one_expert(total, items):
        tokens_of, gate_of, first_weight, second_weight = items
        rows = normed[tokens_of]
        result = jnp.zeros((slot_count, D), jnp.float32)
        for half in range(2):
            hidden = jnp.maximum(jnp.dot(rows, first_weight[half], preferred_element_type=jnp.float32), 0.0).astype(jnp.bfloat16)
            result = result + jnp.dot(hidden, second_weight[half], preferred_element_type=jnp.float32)
        return (total.at[tokens_of].add(gate_of[:, None] * result), None)
    mixture, _ = lax.scan(one_expert, jnp.zeros((total_rows, D), jnp.float32), (slot_token, slot_gate, halves_in, halves_out))
    updated = source_tokens.astype(jnp.float32) + mixture
    memory = (layer_norm(updated) * final_gain).astype(jnp.bfloat16)
    queries = jnp.dot(target_tokens, query_weight, preferred_element_type=jnp.float32).astype(jnp.bfloat16)
    keys = jnp.dot(memory, key_weight, preferred_element_type=jnp.float32).astype(jnp.bfloat16)
    values = jnp.dot(memory, value_weight, preferred_element_type=jnp.float32).astype(jnp.bfloat16)
    keys = keys.reshape(2, N_EXPERT, TOK_DEV, HD)[::-1].reshape(DEVICES, TOK_DEV, HEADS, HDIM)
    values = values.reshape(2, N_EXPERT, TOK_DEV, HD)[::-1].reshape(DEVICES, TOK_DEV, HEADS, HDIM)
    key_sentence = source_sentence.reshape(2, N_EXPERT, TOK_DEV)[::-1].reshape(DEVICES, TOK_DEV)
    queries = queries.reshape(DEVICES, TGT_DEV, HEADS, HDIM)
    scale = 1.0 / HDIM ** 0.5

    def one_block(items):
        query_block, key_block, value_block, query_ids, key_ids = items
        scores = jnp.einsum('qhd,khd->hqk', query_block.astype(jnp.float32), key_block.astype(jnp.float32)) * scale
        same = (query_ids[:, None] == key_ids[None, :])[None, :, :]
        scores = jnp.where(same, scores, -jnp.inf)
        peak = lax.optimization_barrier(jnp.max(scores, axis=-1, keepdims=True))
        raised = jnp.exp(scores - peak)
        probs = (raised / lax.optimization_barrier(jnp.sum(raised, axis=-1, keepdims=True))).astype(jnp.bfloat16)
        mixed = jnp.einsum('hqk,khd->qhd', probs.astype(jnp.float32), value_block.astype(jnp.float32))
        return mixed.reshape(TGT_DEV, HD).astype(jnp.bfloat16)
    context = lax.map(one_block, (queries, keys, values, target_sentence, key_sentence))
    return (memory, context.reshape(TGT_TOKENS, HD))
```

```python
import functools

import jax
import jax.numpy as jnp
from jax import lax
from jax.experimental import pallas as pl
from jax.experimental.pallas import tpu as pltpu
from jax.sharding import PartitionSpec as P

HEADS = 8
HDIM = 128
MESH = pl.DeviceIdType.MESH
CHUNKS = 4
TILE = 256


def layer_norm(values):
    mean = jnp.mean(values, axis=-1, keepdims=True)
    centred = values - mean
    spread = jnp.mean(centred * centred, axis=-1, keepdims=True)
    return centred * lax.rsqrt(spread + 1e-05)


def await_bytes(ref, sem):
    pltpu.make_async_copy(ref, ref, sem).wait()


def expert_kernel(
    packed,
    first,
    second,
    share,
    back,
    gathered,
    rows_in,
    rows,
    w_first,
    w_second,
    hidden,
    result,
    mate_part,
    part_in,
    summed,
    share_in,
    strip,
    d_send,
    d_recv,
    f_send,
    f_recv,
    w_send,
    w_recv,
    w_local,
    p_send,
    p_recv,
    r_send,
    r_recv,
    a_send,
    a_recv,
    c_sem,
):
    s = lax.axis_index("section")
    j = lax.axis_index("expert")
    y, x, z = j // 32, (j // 8) % 4, j % 8
    k = z // 2
    out = 2 * (z % 2) - 1
    mate = z - out
    column = y * 4 + x
    mine = column * 4 + k

    def device(dy, dx, new_z):
        return (s, (((y + dy) % 4) * 4 + (x + dx) % 4) * 8 + new_z)

    def near(q):
        return (z + (0, out, -2 * out, 3 * out)[q] + 8) % 8

    def origin(q):
        return (z + out * q + 8) % 8

    partner = (1 - s, j)
    mate_id = device(0, 0, mate)
    next_id = device(0, 0, origin(1))

    own_first = pltpu.make_async_copy(first.at[0], w_first.at[0], w_local.at[0])
    own_second = pltpu.make_async_copy(second.at[0], w_second.at[0], w_local.at[1])
    own_first.start()
    own_second.start()

    barrier = pltpu.get_barrier_semaphore()
    spread = (0, 1, 2, -2, 3)

    def greet(dy, dx, step):
        pl.semaphore_signal(
            barrier, inc=1, device_id=device(dy, dx, (z + out * step + 8) % 8), device_id_type=MESH
        )

    def greet_column(g, carry):
        for step in spread:
            greet(g // 4, g % 4, step)
        return carry

    lax.fori_loop(1, 16, greet_column, 0)
    for step in spread[1:]:
        greet(0, 0, step)
    pl.semaphore_signal(barrier, inc=1, device_id=mate_id, device_id_type=MESH)
    pl.semaphore_signal(barrier, inc=1, device_id=partner, device_id_type=MESH)
    pl.semaphore_wait(barrier, 81)

    def remote(src, dst, send, recv, to):
        return pltpu.make_async_remote_copy(
            src_ref=src, dst_ref=dst, send_sem=send, recv_sem=recv, device_id=to, device_id_type=MESH
        )

    share_copy = remote(share, share_in, a_send.at[0], a_recv.at[0], mate_id)
    share_copy.start()

    def dispatch(dy, dx, g, q):
        target = near(q)
        expert = (((y + dy) % 4) * 4 + (x + dx) % 4) * 4 + target // 2
        return expert, device(dy, dx, target)

    kept = pltpu.make_async_copy(packed.at[mine], rows_in.at[0, 0, 0], d_recv.at[0])
    kept.start()

    def send_one(dy, dx, g, q):
        expert, to = dispatch(dy, dx, g, q)
        remote(packed.at[expert], rows_in.at[0, g, q], d_send, d_recv.at[g // 4], to).start()

    for q in range(1, 4):
        send_one(0, 0, 0, q)

    def send_column(g, carry):
        for q in range(4):
            send_one(g // 4, g % 4, g, q)
        return carry

    lax.fori_loop(1, 16, send_column, 0)

    w1_copy = remote(first.at[0], w_first.at[1], w_send.at[0], w_recv.at[0], partner)
    w2_copy = remote(second.at[0], w_second.at[1], w_send.at[1], w_recv.at[1], partner)
    w1_copy.start()
    w2_copy.start()

    here = gathered.at[s, y, x]
    plus, minus = (k + out + 4) % 4, (k - out + 4) % 4
    half = strip.shape[1] // 2
    cols = (pl.ds(0, half), pl.ds(half, half))
    xl, xr = (x + 3) % 4, (x + 1) % 4
    yl, yr = (y + 3) % 4, (y + 1) % 4
    ids = {
        "xl": device(0, 3, z),
        "xr": device(0, 1, z),
        "yl": device(3, 0, z),
        "yr": device(1, 0, z),
    }

    def along(ref, n, to):
        return remote(ref, ref, a_send.at[n], a_recv.at[n], to)

    def gather_0():
        share_copy.wait()
        low = jnp.where(z % 2 == 0, share[...], share_in[...])
        high = jnp.where(z % 2 == 0, share_in[...], share[...])
        strip[...] = jnp.concatenate([low, high], axis=0).astype(jnp.bfloat16)
        pltpu.make_async_copy(strip, here.at[k], w_local.at[2]).start()
        remote(strip, here.at[k], a_send.at[1], a_recv.at[1], next_id).start()

    def gather_1():
        await_bytes(here.at[plus], a_recv.at[1])
        along(here.at[plus], 2, mate_id).start()

    def gather_2():
        await_bytes(here.at[minus], a_recv.at[2])
        along(here.at[minus], 3, next_id).start()

    block_a = lambda yy, xx, ks=pl.ds(0, 4): gathered.at[s, yy, xx, ks, :, cols[0]]
    block_b = lambda yy, xx, ks=pl.ds(0, 4): gathered.at[s, yy, xx, ks, :, cols[1]]
    row_a = lambda yy, ks=pl.ds(0, 4): gathered.at[s, yy, :, ks, :, cols[0]]
    row_b = lambda xx, ks=pl.ds(0, 4): gathered.at[s, :, xx, ks, :, cols[1]]
    lo, hi = pl.ds(0, 2), pl.ds(2, 2)

    def gather_3():
        await_bytes(here.at[(k + 2) % 4], a_recv.at[3])
        pltpu.make_async_copy(strip, here.at[k], w_local.at[2]).wait()
        along(block_a(y, x), 4, ids["xr"]).start()
        along(block_a(y, x), 5, ids["xl"]).start()
        along(block_b(y, x), 6, ids["yr"]).start()
        along(block_b(y, x), 7, ids["yl"]).start()

    def gather_4():
        await_bytes(block_a(y, xl), a_recv.at[4])
        along(block_a(y, xl, lo), 8, ids["xr"]).start()
        await_bytes(block_b(yl, x), a_recv.at[6])
        along(block_b(yl, x, lo), 10, ids["yr"]).start()
        await_bytes(block_a(y, xr), a_recv.at[5])
        along(block_a(y, xr, hi), 9, ids["xl"]).start()
        await_bytes(block_b(yr, x), a_recv.at[7])
        along(block_b(yr, x, hi), 11, ids["yl"]).start()

    def gather_5():
        x2, y2 = (x + 2) % 4, (y + 2) % 4
        await_bytes(block_a(y, x2, lo), a_recv.at[8])
        await_bytes(block_a(y, x2, hi), a_recv.at[9])
        along(row_a(y), 12, ids["yr"]).start()
        along(row_a(y), 13, ids["yl"]).start()
        await_bytes(block_b(y2, x, lo), a_recv.at[10])
        await_bytes(block_b(y2, x, hi), a_recv.at[11])
        along(row_b(x), 14, ids["xr"]).start()
        along(row_b(x), 15, ids["xl"]).start()

    def gather_6():
        await_bytes(row_a(yl), a_recv.at[12])
        along(row_a(yl, lo), 16, ids["yr"]).start()
        await_bytes(row_b(xl), a_recv.at[14])
        along(row_b(xl, lo), 18, ids["xr"]).start()
        await_bytes(row_a(yr), a_recv.at[13])
        along(row_a(yr, hi), 17, ids["yl"]).start()
        await_bytes(row_b(xr), a_recv.at[15])
        along(row_b(xr, hi), 19, ids["xl"]).start()

    def gather_7():
        x2, y2 = (x + 2) % 4, (y + 2) % 4
        await_bytes(row_a(y2, lo), a_recv.at[16])
        await_bytes(row_a(y2, hi), a_recv.at[17])
        await_bytes(row_b(x2, lo), a_recv.at[18])
        await_bytes(row_b(x2, hi), a_recv.at[19])
        along(gathered.at[s], 20, partner).start()

    def gather_8():
        await_bytes(gathered.at[1 - s], a_recv.at[20])
        await_bytes(strip, a_send.at[1])
        for n in (2, 3):
            await_bytes(here.at[k], a_send.at[n])
        for n in (4, 5, 6, 7):
            await_bytes(block_a(y, x), a_send.at[n])
        for n in (8, 9, 10, 11):
            await_bytes(block_a(y, x, lo), a_send.at[n])
        for n in (12, 13, 14, 15):
            await_bytes(row_a(y), a_send.at[n])
        for n in (16, 17, 18, 19):
            await_bytes(row_a(y, lo), a_send.at[n])
        await_bytes(gathered.at[s], a_send.at[20])

    groups = 16 // CHUNKS
    count = groups * 4 * 5

    def arrive(c):
        part = pl.ds(c * groups, groups)
        await_bytes(rows_in.at[0, part], d_recv.at[c])
        remote(rows_in.at[0, part], rows_in.at[1, part], f_send, f_recv.at[c], mate_id).start()

    def compute(c):
        part = pl.ds(c * groups, groups)
        await_bytes(rows_in.at[1, part], f_recv.at[c])
        for side in range(2):
            tiles = rows_in[side, part].reshape(count, 16, 128)
            rows[side * count : (side + 1) * count] = tiles.reshape(count, 2048)
        width = w_first.shape[2]

        def up(n, carry):
            for side in range(2):
                at = pl.multiple_of(n * TILE, TILE)
                weight = w_first[side, :, pl.ds(at, TILE)]
                value = jnp.dot(rows[...], weight, preferred_element_type=jnp.float32)
                value = jnp.maximum(value, 0.0).astype(jnp.bfloat16)
                hidden[:, pl.ds(pl.multiple_of(side * width + at, TILE), TILE)] = value
            return carry

        lax.fori_loop(0, width // TILE, up, 0)

        def down(n, carry):
            at = pl.ds(pl.multiple_of(n * TILE, TILE), TILE)
            value = jnp.dot(
                hidden[:, :width], w_second[0, :, at], preferred_element_type=jnp.float32
            ) + jnp.dot(hidden[:, width:], w_second[1, :, at], preferred_element_type=jnp.float32)
            result[:, at] = value.astype(jnp.bfloat16)
            return carry

        lax.fori_loop(0, result.shape[1] // TILE, down, 0)
        shape = (groups, 4, 5, 16, 128)
        mate_part[part] = result[count:].reshape(count, 16, 128).reshape(shape)
        remote(mate_part.at[part], part_in.at[part], p_send, p_recv.at[c], mate_id).start()
        summed[part] = result[:count].reshape(count, 16, 128).reshape(shape)

    def reply(c):
        part = pl.ds(c * groups, groups)
        await_bytes(part_in.at[part], p_recv.at[c])
        total = summed[part].astype(jnp.float32) + part_in[part].astype(jnp.float32)
        summed[part] = total.astype(jnp.bfloat16)

        def send_back(n, carry):
            g = c * groups + n
            for q in range(4):
                to = device(4 - g // 4, 4 - g % 4, origin(q))
                copy = remote(summed.at[g, q], back.at[mine], r_send, r_recv, to)
                if q == 0:

                    @pl.when(g > 0)
                    def _():
                        copy.start()

                    @pl.when(g == 0)
                    def _():
                        pltpu.make_async_copy(summed.at[0, 0], back.at[mine], r_recv).start()

                else:
                    copy.start()
            return carry

        lax.fori_loop(0, groups, send_back, 0)

    steps = (gather_1, gather_2, gather_3, gather_4, gather_5, gather_6)
    gather_0()

    def turn(t, carry):
        for n, step in enumerate(steps):
            pl.when(t == n)(step)
        pl.when(t < CHUNKS)(lambda: arrive(t))

        @pl.when(t == 1)
        def _():
            own_first.wait()
            own_second.wait()
            w1_copy.wait()
            w2_copy.wait()

        pl.when((t >= 1) & (t <= CHUNKS))(lambda: compute(t - 1))
        pl.when(t >= 2)(lambda: reply(t - 2))
        return carry

    lax.fori_loop(0, CHUNKS + 2, turn, 0)
    gather_7()
    await_bytes(back, r_recv)
    await_bytes(back.at[pl.ds(0, 63)], r_send)
    await_bytes(back.at[pl.ds(0, 63)], d_send)
    await_bytes(rows_in.at[0], f_send)
    await_bytes(mate_part, p_send)
    gather_8()


def run_experts(packed, first, second, share):
    bf, f32, dma = jnp.bfloat16, jnp.float32, pltpu.SemaphoreType.DMA
    count = 2 * 320 // CHUNKS
    vmem = pl.BlockSpec(memory_space=pltpu.VMEM)
    hbm = pl.BlockSpec(memory_space=pl.ANY)
    return pl.pallas_call(
        expert_kernel,
        out_shape=(
            jax.ShapeDtypeStruct((64, 5, 16, 128), bf),
            jax.ShapeDtypeStruct((2, 4, 4, 4, 16, 3072), bf),
        ),
        in_specs=[vmem, hbm, hbm, vmem],
        out_specs=(vmem, hbm),
        scratch_shapes=[
            pltpu.VMEM((2, 16, 4, 5, 16, 128), bf),
            pltpu.VMEM((count, 2048), bf),
            pltpu.VMEM((2, 2048, 1024), bf),
            pltpu.VMEM((2, 1024, 2048), bf),
            pltpu.VMEM((count, 2048), bf),
            pltpu.VMEM((count, 2048), bf),
            pltpu.VMEM((16, 4, 5, 16, 128), bf),
            pltpu.VMEM((16, 4, 5, 16, 128), bf),
            pltpu.VMEM((16, 4, 5, 16, 128), bf),
            pltpu.VMEM((8, 3072), f32),
            pltpu.VMEM((16, 3072), bf),
            dma,
            dma((CHUNKS,)),
            dma,
            dma((CHUNKS,)),
            dma((2,)),
            dma((2,)),
            dma((3,)),
            dma,
            dma((CHUNKS,)),
            dma,
            dma,
            dma((21,)),
            dma((21,)),
            dma,
        ],
        compiler_params=pltpu.CompilerParams(
            collective_id=0, has_side_effects=True, vmem_limit_bytes=48 << 20
        ),
        cost_estimate=pl.CostEstimate(
            flops=11 * 10**9, bytes_accessed=40 * 10**6, transcendentals=0
        ),
    )(packed, first, second, share)


def swapped(block, axis):
    return lax.ppermute(block, axis, [(0, 1), (1, 0)])


def body(
    source_tokens,
    routes,
    gates,
    source_sentence,
    expert_in,
    expert_out,
    final_gain,
    target_tokens,
    target_sentence,
    query_weight,
    key_weight,
    value_weight,
):
    experts, capacity = 64, 5
    rows_here, width = source_tokens.shape
    normed = layer_norm(source_tokens.astype(jnp.float32)).astype(jnp.bfloat16)
    flat = routes.reshape(-1)
    picks = (flat[:, None] == jnp.arange(experts, dtype=jnp.int32)[None, :]).astype(jnp.int32)
    places = jnp.sum((jnp.cumsum(picks, axis=0) - 1) * picks, axis=1)
    slot_of = (flat * capacity + places).reshape(rows_here, 2)
    hits = slot_of[:, :, None] == jnp.arange(experts * capacity, dtype=jnp.int32)[None, None, :]
    chosen = (hits[:, 0] | hits[:, 1]).astype(jnp.bfloat16)
    packed = jnp.dot(chosen.T, normed, preferred_element_type=jnp.float32).astype(jnp.bfloat16)
    packed = packed.reshape(experts, capacity, 16, 128)
    share = jnp.concatenate([query_weight, key_weight, value_weight], axis=1).astype(jnp.float32)
    back, gathered = run_experts(packed, expert_in, expert_out, share)
    back = back.reshape(experts * capacity, width)
    weights = gathered.reshape(width, 3072)
    mixing = jnp.sum(jnp.where(hits, gates[:, :, None], 0.0), axis=1)
    high = mixing.astype(jnp.bfloat16)
    low = (mixing - high.astype(jnp.float32)).astype(jnp.bfloat16)
    mixture = jnp.dot(high, back, preferred_element_type=jnp.float32) + jnp.dot(
        low, back, preferred_element_type=jnp.float32
    )
    updated = source_tokens.astype(jnp.float32) + mixture
    memory = (layer_norm(updated) * final_gain).astype(jnp.bfloat16)
    partner_memory, partner_sentence = swapped((memory, source_sentence), "section")
    head_width = query_weight.shape[1]
    target_rows = target_tokens.shape[0]
    key_rows = partner_memory.shape[0]
    queries = jnp.dot(
        target_tokens, weights[:, :head_width], preferred_element_type=jnp.float32
    )
    both = jnp.dot(
        partner_memory, weights[:, head_width:], preferred_element_type=jnp.float32
    ).astype(jnp.bfloat16)
    queries = queries.astype(jnp.bfloat16).reshape(target_rows, HEADS, HDIM)
    keys = both[:, :head_width].reshape(key_rows, HEADS, HDIM)
    values = both[:, head_width:].reshape(key_rows, HEADS, HDIM)
    scores = jnp.einsum("qhd,khd->hqk", queries, keys, preferred_element_type=jnp.float32) * (
        1.0 / HDIM**0.5
    )
    same = (target_sentence[0][:, None] == partner_sentence[0][None, :])[None, :, :]
    scores = jnp.where(same, scores, -jnp.inf)
    peak = jnp.max(scores, axis=-1, keepdims=True)
    raised = jnp.exp(scores - peak)
    probs = (raised / jnp.sum(raised, axis=-1, keepdims=True)).astype(jnp.bfloat16)
    mixed = jnp.einsum("hqk,khd->qhd", probs, values, preferred_element_type=jnp.float32)
    return (memory, mixed.reshape(target_rows, head_width).astype(jnp.bfloat16))


def solution(mesh):
    rows = P(("section", "expert"), None)
    placed = (
        rows,
        rows,
        rows,
        rows,
        P("expert", None, "section"),
        P("expert", "section", None),
        P(),
        rows,
        rows,
        rows,
        rows,
        rows,
    )
    return jax.shard_map(
        body, mesh=mesh, in_specs=placed, out_specs=(rows, rows), check_vma=False
    )
```

```python
import jax
import jax.numpy as jnp
from jax import lax
from jax.experimental import pallas as pl
from jax.experimental.pallas import tpu as pltpu
from jax.sharding import PartitionSpec as P

HDIM = 128
MESH = pl.DeviceIdType.MESH
CHUNKS = 4
TILE = 256
PLAN = {"norm": ((0, 0),), "route": ((0, 1),), "first": ((0, 2),), "arrived": ((0, 3), (1, 4), (2, 5)), "replied": ((3, 6), (5, 7))}


def layer_norm(values):
    mean = jnp.mean(values, axis=-1, keepdims=True)
    centred = values - mean
    spread = jnp.mean(centred * centred, axis=-1, keepdims=True)
    return centred * lax.rsqrt(spread + 1e-05)


def await_bytes(ref, sem):
    pltpu.make_async_copy(ref, ref, sem).wait()


def layer_kernel(
    source,
    routes,
    gates,
    sentence,
    first,
    second,
    gain,
    target,
    target_sentence,
    wq,
    wk,
    wv,
    memory,
    context,
    normed,
    picked,
    mixing,
    packed,
    rows_in,
    rows,
    w_first,
    w_second,
    hidden,
    result,
    mate_part,
    part_in,
    summed,
    share,
    share_in,
    gathered,
    back,
    straight,
    updated,
    targets,
    queries,
    kv,
    kv_in,
    sentence_in,
    d_send,
    d_recv,
    f_send,
    f_recv,
    w_send,
    w_recv,
    w_local,
    p_send,
    p_recv,
    r_send,
    r_recv,
    a_send,
    a_recv,
    x_send,
    x_recv,
    k_send,
    k_recv,
    s_sem,
):
    f32, bf = jnp.float32, jnp.bfloat16
    s = lax.axis_index("section")
    j = lax.axis_index("expert")
    y, x, z = j // 32, (j // 8) % 4, j % 8
    k = z // 2
    out = 2 * (z % 2) - 1
    mate = z - out
    mine = (y * 4 + x) * 4 + k

    def device(dy, dx, new_z):
        return (s, (((y + dy) % 4) * 4 + (x + dx) % 4) * 8 + new_z)

    def near(q):
        return (z + (0, out, -2 * out, 3 * out)[q] + 8) % 8

    def origin(q):
        return (z + out * q + 8) % 8

    partner = (1 - s, j)
    mate_id = device(0, 0, mate)
    next_id = device(0, 0, origin(1))

    own_first = pltpu.make_async_copy(first.at[0], w_first.at[0], w_local.at[0])
    own_second = pltpu.make_async_copy(second.at[0], w_second.at[0], w_local.at[1])
    own_target = pltpu.make_async_copy(target, targets, w_local.at[2])
    own_first.start()
    own_second.start()
    own_target.start()

    barrier = pltpu.get_barrier_semaphore()
    spread = (0, 1, 2, -2, 3)

    def greet(dy, dx, step):
        pl.semaphore_signal(
            barrier, inc=1, device_id=device(dy, dx, (z + out * step + 8) % 8), device_id_type=MESH
        )

    def greet_column(g, carry):
        for step in spread:
            greet(g // 4, g % 4, step)
        return carry

    lax.fori_loop(1, 16, greet_column, 0)
    for step in spread[1:]:
        greet(0, 0, step)
    pl.semaphore_signal(barrier, inc=1, device_id=mate_id, device_id_type=MESH)
    pl.semaphore_signal(barrier, inc=1, device_id=partner, device_id_type=MESH)
    for n, part in enumerate((wq, wk, wv)):
        share[:, n * 1024 : (n + 1) * 1024] = part[...].astype(f32)
    pl.semaphore_wait(barrier, 81)

    def remote(src, dst, send, recv, to):
        return pltpu.make_async_remote_copy(
            src_ref=src, dst_ref=dst, send_sem=send, recv_sem=recv, device_id=to, device_id_type=MESH
        )

    share_copy = remote(share, share_in, a_send.at[0], a_recv.at[0], mate_id)
    share_copy.start()
    sentence_copy = remote(sentence, sentence_in, s_sem.at[0], s_sem.at[1], partner)
    sentence_copy.start()
    w1_copy = remote(first.at[0], w_first.at[1], w_send.at[0], w_recv.at[0], partner)
    w2_copy = remote(second.at[0], w_second.at[1], w_send.at[1], w_recv.at[1], partner)
    w1_copy.start()
    w2_copy.start()

    here = gathered.at[s, y, x]
    plus, minus = (k + out + 4) % 4, (k - out + 4) % 4
    half = gathered.shape[5] // 2
    cols = (pl.ds(0, half), pl.ds(half, half))
    xl, xr = (x + 3) % 4, (x + 1) % 4
    yl, yr = (y + 3) % 4, (y + 1) % 4
    x2, y2 = (x + 2) % 4, (y + 2) % 4
    id_xl, id_xr = device(0, 3, z), device(0, 1, z)
    id_yl, id_yr = device(3, 0, z), device(1, 0, z)
    every, lo, hi = pl.ds(0, 4), pl.ds(0, 2), pl.ds(2, 2)

    def along(ref, n, to):
        remote(ref, ref, a_send.at[n], a_recv.at[n], to).start()

    def across(ref):
        remote(ref, ref, x_send, x_recv, partner).start()

    def block_a(yy, xx, ks=every):
        return gathered.at[s, yy, xx, ks, :, cols[0]]

    def block_b(yy, xx, ks=every):
        return gathered.at[s, yy, xx, ks, :, cols[1]]

    def row_a(yy, ks=every):
        return gathered.at[s, yy, :, ks, :, cols[0]]

    def row_b(xx, ks=every):
        return gathered.at[s, :, xx, ks, :, cols[1]]

    def gather_0():
        share_copy.wait()
        low = jnp.where(z % 2 == 0, share[...], share_in[...])
        high = jnp.where(z % 2 == 0, share_in[...], share[...])
        gathered[s, y, x, k] = jnp.concatenate([low, high], axis=0).astype(bf)
        along(here.at[k], 1, next_id)

    def gather_1():
        await_bytes(here.at[plus], a_recv.at[1])
        along(here.at[plus], 2, mate_id)

    def gather_2():
        await_bytes(here.at[minus], a_recv.at[2])
        along(here.at[minus], 3, next_id)

    def gather_3():
        await_bytes(here.at[(k + 2) % 4], a_recv.at[3])
        along(block_a(y, x), 4, id_xr)
        along(block_b(y, x), 6, id_yr)
        along(block_a(y, x), 5, id_xl)
        along(block_b(y, x), 7, id_yl)
        across(here)

    def gather_4():
        await_bytes(block_a(y, xl), a_recv.at[4])
        along(block_a(y, xl, lo), 8, id_xr)
        await_bytes(block_b(yl, x), a_recv.at[6])
        along(block_b(yl, x, lo), 10, id_yr)
        await_bytes(block_a(y, xr), a_recv.at[5])
        along(block_a(y, xr, hi), 9, id_xl)
        await_bytes(block_b(yr, x), a_recv.at[7])
        along(block_b(yr, x, hi), 11, id_yl)
        for ref in (block_a(y, xl), block_b(yl, x), block_a(y, xr), block_b(yr, x)):
            across(ref)

    def gather_5():
        await_bytes(block_a(y, x2, lo), a_recv.at[8])
        await_bytes(block_a(y, x2, hi), a_recv.at[9])
        along(row_a(y), 12, id_yr)
        along(row_a(y), 13, id_yl)
        await_bytes(block_b(y2, x, lo), a_recv.at[10])
        await_bytes(block_b(y2, x, hi), a_recv.at[11])
        along(row_b(x), 14, id_xr)
        along(row_b(x), 15, id_xl)
        across(block_a(y, x2))
        across(block_b(y2, x))

    def gather_6():
        await_bytes(row_a(yl), a_recv.at[12])
        along(row_a(yl, lo), 16, id_yr)
        await_bytes(row_b(xl), a_recv.at[14])
        along(row_b(xl, lo), 18, id_xr)
        await_bytes(row_a(yr), a_recv.at[13])
        along(row_a(yr, hi), 17, id_yl)
        await_bytes(row_b(xr), a_recv.at[15])
        along(row_b(xr, hi), 19, id_xl)
        for ref in (row_a(yl), row_b(xl), row_a(yr), row_b(xr)):
            across(ref)

    def gather_7():
        await_bytes(row_a(y2, lo), a_recv.at[16])
        await_bytes(row_a(y2, hi), a_recv.at[17])
        across(row_a(y2))
        await_bytes(row_b(x2, lo), a_recv.at[18])
        await_bytes(row_b(x2, hi), a_recv.at[19])
        across(row_b(x2))

    def gather_done():
        for n in (1, 2, 3):
            await_bytes(here.at[k], a_send.at[n])
        for n in range(4, 8):
            await_bytes(block_a(y, x), a_send.at[n])
        for n in range(8, 12):
            await_bytes(block_a(y, x, lo), a_send.at[n])
        for n in range(12, 16):
            await_bytes(row_a(y), a_send.at[n])
        for n in range(16, 20):
            await_bytes(row_a(y, lo), a_send.at[n])
        await_bytes(gathered.at[s], x_send)

    steps = (gather_0, gather_1, gather_2, gather_3, gather_4, gather_5, gather_6, gather_7)

    def gather(place, t=None):
        for when, step in PLAN.get(place, ()):
            if t is None:
                steps[step]()
            else:
                pl.when(t == when)(steps[step])

    count_t, width = source.shape
    normed[...] = layer_norm(source[...].astype(f32)).astype(bf)
    gather("norm")
    token = lax.broadcasted_iota(jnp.int32, (128, count_t), 1)
    expert = lax.broadcasted_iota(jnp.int32, (128, count_t), 0)
    pick_0 = (routes[0:1, :] == expert).astype(f32)
    pick_1 = (routes[1:2, :] == expert).astype(f32)
    picks = pick_0 + pick_1
    earlier = (expert < token).astype(bf)
    before = jnp.dot(picks.astype(bf), earlier, preferred_element_type=f32)
    slots = packed.shape[0] * packed.shape[1]
    slot = lax.broadcasted_iota(jnp.int32, (picked.shape[0], 128), 0)
    owner = lax.broadcasted_iota(jnp.int32, (picked.shape[0], 128), 1)
    wide = ((slot >= owner * 5) & (slot < owner * 5 + 5)).astype(bf)

    def widen(value):
        return jnp.dot(wide, value.astype(bf), preferred_element_type=f32)

    slot_f = slot.astype(f32)
    place = slot_f - 5.0 * jnp.floor((slot_f + 0.5) * 0.2)
    hits = widen(picks) * (widen(before) == place).astype(f32)
    picked[...] = hits.astype(bf)
    weight = pick_0 * gates[0:1, :] + pick_1 * gates[1:2, :]
    weight_high = weight.astype(bf).astype(f32)
    mixing[0] = (hits * widen(weight_high)).T[:, :slots].astype(bf)
    mixing[1] = (hits * widen(weight - weight_high)).T[:, :slots].astype(bf)
    gather("route")

    kept = pltpu.make_async_copy(packed.at[mine], rows_in.at[0, 0, 0], d_recv.at[0])

    def send_one(dy, dx, q):
        g = dy * 4 + dx
        goal = near(q)
        expert = (((y + dy) % 4) * 4 + (x + dx) % 4) * 4 + goal // 2
        remote(
            packed.at[expert], rows_in.at[0, g, q], d_send, d_recv.at[g], device(dy, dx, goal)
        ).start()

    for dy in range(4):
        block = (y + dy) % 4
        chosen = picked[pl.ds(pl.multiple_of(block * 80, 16), 80), :]
        rows80 = jnp.dot(chosen, normed[...], preferred_element_type=f32).astype(bf)
        packed[pl.ds(block * 16, 16)] = rows80.reshape(80, 16, 128).reshape(16, 5, 16, 128)
        if dy == 0:
            kept.start()
            for q in (2, 3, 1):
                send_one(0, 0, q)

        def send_dx(dx, carry):
            for q in (2, 3, 1, 0):
                send_one(dy, dx, q)
            return carry

        lax.fori_loop(1 if dy == 0 else 0, 4, send_dx, 0)
        if dy == 0:
            gather("first")
    gather("sent")

    groups = 16 // CHUNKS
    count = groups * 4 * 5

    def arrive(c):
        def one(n, carry):
            g = c * groups + n
            await_bytes(rows_in.at[0, g], d_recv.at[g])
            remote(rows_in.at[0, g], rows_in.at[1, g], f_send, f_recv.at[c], mate_id).start()
            return carry

        lax.fori_loop(0, groups, one, 0)

    def compute(c):
        part = pl.ds(c * groups, groups)
        await_bytes(rows_in.at[1, part], f_recv.at[c])
        for side in range(2):
            tiles = rows_in[side, part].reshape(count, 16, 128)
            rows[side * count : (side + 1) * count] = tiles.reshape(count, width)
        depth = w_first.shape[2]

        def up(n, carry):
            for side in range(2):
                at = pl.multiple_of(n * TILE, TILE)
                value = jnp.dot(
                    rows[...], w_first[side, :, pl.ds(at, TILE)], preferred_element_type=f32
                )
                value = jnp.maximum(value, 0.0).astype(bf)
                hidden[:, pl.ds(pl.multiple_of(side * depth + at, TILE), TILE)] = value
            return carry

        lax.fori_loop(0, depth // TILE, up, 0)

        def down(n, carry):
            at = pl.ds(pl.multiple_of(n * TILE, TILE), TILE)
            value = jnp.dot(
                hidden[:, :depth], w_second[0, :, at], preferred_element_type=f32
            ) + jnp.dot(hidden[:, depth:], w_second[1, :, at], preferred_element_type=f32)
            result[:, at] = value.astype(bf)
            return carry

        lax.fori_loop(0, width // TILE, down, 0)
        shape = (groups, 4, 5, 16, 128)
        mate_part[part] = result[count:].reshape(count, 16, 128).reshape(shape)
        remote(mate_part.at[part], part_in.at[part], p_send, p_recv.at[c], mate_id).start()
        summed[part] = result[:count].reshape(count, 16, 128).reshape(shape)

    def reply(c):
        part = pl.ds(c * groups, groups)
        await_bytes(part_in.at[part], p_recv.at[c])
        total = summed[part].astype(f32) + part_in[part].astype(f32)
        summed[part] = total.astype(bf)

        def send_back(n, carry):
            g = c * groups + n
            for q in (2, 3, 1, 0):
                to = device(4 - g // 4, 4 - g % 4, origin(q))
                copy = remote(summed.at[g, q], back.at[mine], r_send, r_recv, to)
                if q == 0:

                    @pl.when(g > 0)
                    def _():
                        copy.start()

                    @pl.when(g == 0)
                    def _():
                        pltpu.make_async_copy(summed.at[0, 0], back.at[mine], r_recv).start()

                else:
                    copy.start()
            return carry

        lax.fori_loop(0, groups, send_back, 0)

    def turn(t, carry):
        gather("turn", t)
        pl.when(t < CHUNKS)(lambda: arrive(t))
        gather("arrived", t)

        @pl.when(t == 1)
        def _():
            own_first.wait()
            own_second.wait()
            w1_copy.wait()
            w2_copy.wait()

        pl.when((t >= 1) & (t <= CHUNKS))(lambda: compute(t - 1))
        gather("computed", t)
        pl.when(t >= 2)(lambda: reply(t - 2))
        gather("replied", t)
        return carry

    lax.fori_loop(0, CHUNKS + 2, turn, 0)
    gather("end")

    own_target.wait()
    sentence_copy.wait()
    await_bytes(gathered.at[1 - s], x_recv)

    def weight_tile(at):
        return gathered[:, :, :, :, :, pl.ds(pl.multiple_of(at, TILE), TILE)].reshape(width, TILE)

    def query(n, carry):
        value = jnp.dot(targets[...], weight_tile(n * TILE), preferred_element_type=f32)
        queries[:, pl.ds(pl.multiple_of(n * TILE, TILE), TILE)] = value.astype(bf)
        return carry

    lax.fori_loop(0, 1024 // TILE, query, 0)
    target_rows = targets.shape[0]
    ids = jnp.broadcast_to(target_sentence[...].astype(f32), (128, target_rows)).T
    same = ids == sentence_in[...].astype(f32)

    await_bytes(back, r_recv)

    def straighten(n, carry):
        tiles = back[pl.ds(n * 16, 16)].reshape(80, 16, 128)
        straight[pl.ds(pl.multiple_of(n * 80, 16), 80), :] = tiles.reshape(80, width)
        return carry

    lax.fori_loop(0, 4, straighten, 0)

    def mix(n, carry):
        at = pl.ds(pl.multiple_of(n * TILE, TILE), TILE)
        part = straight[:, at]
        value = jnp.dot(mixing[0], part, preferred_element_type=f32) + jnp.dot(
            mixing[1], part, preferred_element_type=f32
        )
        updated[:, at] = source[:, at].astype(f32) + value
        return carry

    lax.fori_loop(0, width // TILE, mix, 0)
    memory[...] = (layer_norm(updated[...]) * gain[...]).astype(bf)

    def project(n, carry):
        for side in range(2):
            value = jnp.dot(
                memory[...],
                weight_tile(1024 * (side + 1) + n * TILE),
                preferred_element_type=f32,
            )
            kv[n, side] = value.astype(bf)
        remote(kv.at[n], kv_in.at[n], k_send, k_recv.at[n], partner).start()
        return carry

    lax.fori_loop(0, 4, project, 0)

    def attend(n, carry):
        await_bytes(kv_in.at[n], k_recv.at[n])
        for side in range(TILE // HDIM):
            inner = slice(side * HDIM, (side + 1) * HDIM)
            at = pl.ds(pl.multiple_of(n * TILE + side * HDIM, HDIM), HDIM)
            scores = lax.dot_general(
                queries[:, at],
                kv_in[n, 0, :, inner],
                (((1,), (1,)), ((), ())),
                preferred_element_type=f32,
            ) * (1.0 / HDIM**0.5)
            scores = jnp.where(same, scores, -jnp.inf)
            peak = jnp.max(scores, axis=-1, keepdims=True)
            raised = jnp.exp(scores - peak)
            probs = (raised / jnp.sum(raised, axis=-1, keepdims=True)).astype(bf)
            mixed = jnp.dot(probs, kv_in[n, 1, :, inner], preferred_element_type=f32)
            context[:, at] = mixed.astype(bf)
        return carry

    lax.fori_loop(0, 4, attend, 0)
    await_bytes(kv, k_send)
    await_bytes(back.at[pl.ds(0, 63)], r_send)
    await_bytes(back.at[pl.ds(0, 63)], d_send)
    await_bytes(rows_in.at[0], f_send)
    await_bytes(mate_part, p_send)
    gather_done()


def hand_over(memory, context, memory_out, context_out, sem):
    copies = (
        pltpu.make_async_copy(memory, memory_out, sem.at[0]),
        pltpu.make_async_copy(context, context_out, sem.at[1]),
    )
    for copy in copies:
        copy.start()
    for copy in copies:
        copy.wait()


def body(
    source_tokens,
    routes,
    gates,
    source_sentence,
    expert_in,
    expert_out,
    final_gain,
    target_tokens,
    target_sentence,
    query_weight,
    key_weight,
    value_weight,
):
    bf, f32, dma = jnp.bfloat16, jnp.float32, pltpu.SemaphoreType.DMA
    rows, width = source_tokens.shape
    target_rows = target_tokens.shape[0]
    count = 2 * 320 // CHUNKS
    vmem = pl.BlockSpec(memory_space=pltpu.VMEM)
    hbm = pl.BlockSpec(memory_space=pl.ANY)
    results = pl.pallas_call(
        layer_kernel,
        out_shape=(
            jax.ShapeDtypeStruct((rows, width), bf),
            jax.ShapeDtypeStruct((target_rows, 1024), bf),
        ),
        in_specs=[vmem, vmem, vmem, vmem, hbm, hbm, vmem, hbm, vmem, vmem, vmem, vmem],
        out_specs=(vmem, vmem),
        scratch_shapes=[
            pltpu.VMEM((rows, width), bf),
            pltpu.VMEM((384, rows), bf),
            pltpu.VMEM((2, rows, 320), bf),
            pltpu.VMEM((64, 5, 16, 128), bf),
            pltpu.VMEM((2, 16, 4, 5, 16, 128), bf),
            pltpu.VMEM((count, width), bf),
            pltpu.VMEM((2, width, 1024), bf),
            pltpu.VMEM((2, 1024, width), bf),
            pltpu.VMEM((count, width), bf),
            pltpu.VMEM((count, width), bf),
            pltpu.VMEM((16, 4, 5, 16, 128), bf),
            pltpu.VMEM((16, 4, 5, 16, 128), bf),
            pltpu.VMEM((16, 4, 5, 16, 128), bf),
            pltpu.VMEM((8, 3072), f32),
            pltpu.VMEM((8, 3072), f32),
            pltpu.VMEM((2, 4, 4, 4, 16, 3072), bf),
            pltpu.VMEM((64, 5, 16, 128), bf),
            pltpu.VMEM((320, width), bf),
            pltpu.VMEM((rows, width), f32),
            pltpu.VMEM((target_rows, width), bf),
            pltpu.VMEM((target_rows, 1024), bf),
            pltpu.VMEM((4, 2, rows, TILE), bf),
            pltpu.VMEM((4, 2, rows, TILE), bf),
            pltpu.VMEM((1, rows), jnp.int32),
            dma,
            dma((16,)),
            dma,
            dma((CHUNKS,)),
            dma((2,)),
            dma((2,)),
            dma((3,)),
            dma,
            dma((CHUNKS,)),
            dma,
            dma,
            dma((20,)),
            dma((20,)),
            dma,
            dma,
            dma,
            dma((4,)),
            dma((2,)),
        ],
        compiler_params=pltpu.CompilerParams(
            collective_id=0, has_side_effects=True, vmem_limit_bytes=58 << 20
        ),
        cost_estimate=pl.CostEstimate(
            flops=13 * 10**9, bytes_accessed=20 * 10**6, transcendentals=0
        ),
    )(
        source_tokens,
        routes.T,
        gates.T,
        source_sentence,
        expert_in,
        expert_out,
        final_gain.reshape(1, width),
        target_tokens,
        target_sentence,
        query_weight,
        key_weight,
        value_weight,
    )
    return pl.pallas_call(
        hand_over,
        out_shape=tuple(jax.ShapeDtypeStruct(part.shape, part.dtype) for part in results),
        in_specs=[vmem, vmem],
        out_specs=(hbm, hbm),
        scratch_shapes=[dma((2,))],
    )(*results)


def solution(mesh):
    rows = P(("section", "expert"), None)
    placed = (
        rows,
        rows,
        rows,
        rows,
        P("expert", None, "section"),
        P("expert", "section", None),
        P(),
        rows,
        rows,
        rows,
        rows,
        rows,
    )
    return jax.shard_map(
        body, mesh=mesh, in_specs=placed, out_specs=(rows, rows), check_vma=False
    )
```

```python
import jax
import jax.numpy as jnp
from jax import lax
from jax.experimental import pallas as pl
from jax.experimental.pallas import tpu as pltpu
from jax.sharding import PartitionSpec as P

HDIM = 128
MESH = pl.DeviceIdType.MESH
CHUNKS = 4
TILE = 256
PLAN = {"norm": ((0, 0),), "route": ((0, 1),), "first": ((0, 2),), "arrived": ((0, 3), (1, 4)), "computed": ((1, 5), (3, 6), (4, 7))}


def layer_norm(values):
    mean = jnp.mean(values, axis=-1, keepdims=True)
    centred = values - mean
    spread = jnp.mean(centred * centred, axis=-1, keepdims=True)
    return centred * lax.rsqrt(spread + 1e-05)


def await_bytes(ref, sem):
    pltpu.make_async_copy(ref, ref, sem).wait()


def layer_kernel(
    source,
    routes,
    gates,
    sentence,
    first,
    second,
    gain,
    target,
    target_sentence,
    wq,
    wk,
    wv,
    memory_out,
    context_out,
    memory,
    context,
    normed,
    picked,
    mixing,
    packed,
    rows_in,
    rows,
    w_first,
    w_second,
    hidden,
    result,
    mate_part,
    part_in,
    summed,
    share,
    share_in,
    gathered,
    back,
    straight,
    updated,
    targets,
    queries,
    kv,
    kv_in,
    sentence_in,
    d_send,
    d_recv,
    f_send,
    f_recv,
    w_send,
    w_recv,
    w_local,
    p_send,
    p_recv,
    r_send,
    r_recv,
    a_send,
    a_recv,
    x_send,
    x_recv,
    k_send,
    k_recv,
    s_sem,
    o_sem,
):
    f32, bf = jnp.float32, jnp.bfloat16
    s = lax.axis_index("section")
    j = lax.axis_index("expert")
    y, x, z = j // 32, (j // 8) % 4, j % 8
    k = z // 2
    out = 2 * (z % 2) - 1
    mate = z - out
    mine = (y * 4 + x) * 4 + k

    def device(dy, dx, new_z):
        return (s, (((y + dy) % 4) * 4 + (x + dx) % 4) * 8 + new_z)

    def near(q):
        return (z + (0, out, -2 * out, 3 * out)[q] + 8) % 8

    def origin(q):
        return (z + out * q + 8) % 8

    partner = (1 - s, j)
    mate_id = device(0, 0, mate)
    next_id = device(0, 0, origin(1))

    own_first = pltpu.make_async_copy(first.at[0], w_first.at[0], w_local.at[0])
    own_second = pltpu.make_async_copy(second.at[0], w_second.at[0], w_local.at[1])
    own_target = pltpu.make_async_copy(target, targets, w_local.at[2])
    own_first.start()
    own_second.start()
    own_target.start()

    barrier = pltpu.get_barrier_semaphore()
    spread = (0, 1, 2, -2, 3)

    def greet(dy, dx, step):
        pl.semaphore_signal(
            barrier, inc=1, device_id=device(dy, dx, (z + out * step + 8) % 8), device_id_type=MESH
        )

    def greet_column(g, carry):
        for step in spread:
            greet(g // 4, g % 4, step)
        return carry

    lax.fori_loop(1, 16, greet_column, 0)
    for step in spread[1:]:
        greet(0, 0, step)
    pl.semaphore_signal(barrier, inc=1, device_id=mate_id, device_id_type=MESH)
    pl.semaphore_signal(barrier, inc=1, device_id=partner, device_id_type=MESH)
    for n, part in enumerate((wq, wk, wv)):
        share[:, n * 1024 : (n + 1) * 1024] = part[...].astype(f32)
    count_t, width = source.shape
    normed[...] = layer_norm(source[...].astype(f32)).astype(bf)
    token = lax.broadcasted_iota(jnp.int32, (128, count_t), 1)
    expert = lax.broadcasted_iota(jnp.int32, (128, count_t), 0)
    pick_0 = (routes[0:1, :] == expert).astype(f32)
    pick_1 = (routes[1:2, :] == expert).astype(f32)
    picks = pick_0 + pick_1
    earlier = (expert < token).astype(bf)
    before = jnp.dot(picks.astype(bf), earlier, preferred_element_type=f32)
    slot = lax.broadcasted_iota(jnp.int32, (picked.shape[0], 128), 0)
    owner = lax.broadcasted_iota(jnp.int32, (picked.shape[0], 128), 1)
    wide = ((slot >= owner * 5) & (slot < owner * 5 + 5)).astype(bf)

    def widen(value):
        return jnp.dot(wide, value.astype(bf), preferred_element_type=f32)

    slot_f = slot.astype(f32)
    place = slot_f - 5.0 * jnp.floor((slot_f + 0.5) * 0.2)
    hits = widen(picks) * (widen(before) == place).astype(f32)
    picked[...] = hits.astype(bf)
    weight = pick_0 * gates[0:1, :] + pick_1 * gates[1:2, :]
    weight_high = weight.astype(bf).astype(f32)
    for n, part in enumerate((weight_high, weight - weight_high)):
        mixed = (hits * widen(part)).T.astype(bf)
        for block in range(4):
            mixing[n, block] = mixed[:, block * 80 : (block + 1) * 80]

    pl.semaphore_wait(barrier, 81)

    def remote(src, dst, send, recv, to):
        return pltpu.make_async_remote_copy(
            src_ref=src, dst_ref=dst, send_sem=send, recv_sem=recv, device_id=to, device_id_type=MESH
        )

    share_copy = remote(share, share_in, a_send.at[0], a_recv.at[0], mate_id)
    share_copy.start()
    sentence_copy = remote(sentence, sentence_in, s_sem.at[0], s_sem.at[1], partner)
    sentence_copy.start()
    w1_copy = remote(first.at[0], w_first.at[1], w_send.at[0], w_recv.at[0], partner)
    w2_copy = remote(second.at[0], w_second.at[1], w_send.at[1], w_recv.at[1], partner)
    w1_copy.start()
    w2_copy.start()

    here = gathered.at[s, y, x]
    plus, minus = (k + out + 4) % 4, (k - out + 4) % 4
    half = gathered.shape[5] // 2
    cols = (pl.ds(0, half), pl.ds(half, half))
    xl, xr = (x + 3) % 4, (x + 1) % 4
    yl, yr = (y + 3) % 4, (y + 1) % 4
    x2, y2 = (x + 2) % 4, (y + 2) % 4
    id_xl, id_xr = device(0, 3, z), device(0, 1, z)
    id_yl, id_yr = device(3, 0, z), device(1, 0, z)
    every, lo, hi = pl.ds(0, 4), pl.ds(0, 2), pl.ds(2, 2)

    def along(ref, n, to):
        remote(ref, ref, a_send.at[n], a_recv.at[n], to).start()

    def across(ref):
        remote(ref, ref, x_send, x_recv, partner).start()

    def block_a(yy, xx, ks=every):
        return gathered.at[s, yy, xx, ks, :, cols[0]]

    def block_b(yy, xx, ks=every):
        return gathered.at[s, yy, xx, ks, :, cols[1]]

    def row_a(yy, ks=every):
        return gathered.at[s, yy, :, ks, :, cols[0]]

    def row_b(xx, ks=every):
        return gathered.at[s, :, xx, ks, :, cols[1]]

    def gather_0():
        share_copy.wait()
        low = jnp.where(z % 2 == 0, share[...], share_in[...])
        high = jnp.where(z % 2 == 0, share_in[...], share[...])
        gathered[s, y, x, k] = jnp.concatenate([low, high], axis=0).astype(bf)
        along(here.at[k], 1, next_id)

    def gather_1():
        await_bytes(here.at[plus], a_recv.at[1])
        along(here.at[plus], 2, mate_id)

    def gather_2():
        await_bytes(here.at[minus], a_recv.at[2])
        along(here.at[minus], 3, next_id)

    def gather_3():
        await_bytes(here.at[(k + 2) % 4], a_recv.at[3])
        along(block_a(y, x), 4, id_xr)
        along(block_b(y, x), 6, id_yr)
        along(block_a(y, x), 5, id_xl)
        along(block_b(y, x), 7, id_yl)
        across(here)

    def gather_4():
        await_bytes(block_a(y, xl), a_recv.at[4])
        along(block_a(y, xl, lo), 8, id_xr)
        await_bytes(block_b(yl, x), a_recv.at[6])
        along(block_b(yl, x, lo), 10, id_yr)
        await_bytes(block_a(y, xr), a_recv.at[5])
        along(block_a(y, xr, hi), 9, id_xl)
        await_bytes(block_b(yr, x), a_recv.at[7])
        along(block_b(yr, x, hi), 11, id_yl)
        for ref in (block_a(y, xl), block_b(yl, x), block_a(y, xr), block_b(yr, x)):
            across(ref)

    def gather_5():
        await_bytes(block_a(y, x2, lo), a_recv.at[8])
        await_bytes(block_a(y, x2, hi), a_recv.at[9])
        along(row_a(y), 12, id_yr)
        along(row_a(y), 13, id_yl)
        await_bytes(block_b(y2, x, lo), a_recv.at[10])
        await_bytes(block_b(y2, x, hi), a_recv.at[11])
        along(row_b(x), 14, id_xr)
        along(row_b(x), 15, id_xl)
        across(block_a(y, x2))
        across(block_b(y2, x))

    def gather_6():
        await_bytes(row_a(yl), a_recv.at[12])
        along(row_a(yl, lo), 16, id_yr)
        await_bytes(row_b(xl), a_recv.at[14])
        along(row_b(xl, lo), 18, id_xr)
        await_bytes(row_a(yr), a_recv.at[13])
        along(row_a(yr, hi), 17, id_yl)
        await_bytes(row_b(xr), a_recv.at[15])
        along(row_b(xr, hi), 19, id_xl)
        for ref in (row_a(yl), row_b(xl), row_a(yr), row_b(xr)):
            across(ref)

    def gather_7():
        await_bytes(row_a(y2, lo), a_recv.at[16])
        await_bytes(row_a(y2, hi), a_recv.at[17])
        across(row_a(y2))
        await_bytes(row_b(x2, lo), a_recv.at[18])
        await_bytes(row_b(x2, hi), a_recv.at[19])
        across(row_b(x2))

    def gather_done():
        for n in (1, 2, 3):
            await_bytes(here.at[k], a_send.at[n])
        for n in range(4, 8):
            await_bytes(block_a(y, x), a_send.at[n])
        for n in range(8, 12):
            await_bytes(block_a(y, x, lo), a_send.at[n])
        for n in range(12, 16):
            await_bytes(row_a(y), a_send.at[n])
        for n in range(16, 20):
            await_bytes(row_a(y, lo), a_send.at[n])
        await_bytes(gathered.at[s], x_send)

    steps = (gather_0, gather_1, gather_2, gather_3, gather_4, gather_5, gather_6, gather_7)

    def gather(place, t=None):
        for when, step in PLAN.get(place, ()):
            if t is None:
                steps[step]()
            else:
                pl.when(t == when)(steps[step])

    gather("norm")
    gather("route")

    kept = pltpu.make_async_copy(packed.at[mine], rows_in.at[0, 0, 0], d_recv.at[0])

    def send_one(dy, dx, q):
        g = dy * 4 + dx
        goal = near(q)
        expert = (((y + dy) % 4) * 4 + (x + dx) % 4) * 4 + goal // 2
        remote(
            packed.at[expert], rows_in.at[0, g, q], d_send, d_recv.at[g], device(dy, dx, goal)
        ).start()

    for dy in range(4):
        block = (y + dy) % 4
        chosen = picked[pl.ds(pl.multiple_of(block * 80, 16), 80), :]
        rows80 = jnp.dot(chosen, normed[...], preferred_element_type=f32).astype(bf)
        packed[pl.ds(block * 16, 16)] = rows80.reshape(80, 16, 128).reshape(16, 5, 16, 128)
        if dy == 0:
            kept.start()
            for q in (2, 3, 1):
                send_one(0, 0, q)

        def send_dx(dx, carry):
            for q in (2, 3, 1, 0):
                send_one(dy, dx, q)
            return carry

        lax.fori_loop(1 if dy == 0 else 0, 4, send_dx, 0)
        if dy == 0:
            gather("first")
    gather("sent")

    groups = 16 // CHUNKS
    count = groups * 4 * 5

    def arrive(c):
        def one(n, carry):
            g = c * groups + n
            await_bytes(rows_in.at[0, g], d_recv.at[g])
            remote(rows_in.at[0, g], rows_in.at[1, g], f_send, f_recv.at[c], mate_id).start()
            return carry

        lax.fori_loop(0, groups, one, 0)

    def compute(c):
        part = pl.ds(c * groups, groups)
        await_bytes(rows_in.at[1, part], f_recv.at[c])
        tiles = rows_in[:, part].reshape(2 * count, 16, 128)
        rows[...] = tiles.reshape(2 * count, width)
        depth = w_first.shape[2]

        def up(n, carry):
            for side in range(2):
                at = pl.multiple_of(n * TILE, TILE)
                value = jnp.dot(
                    rows[...], w_first[side, :, pl.ds(at, TILE)], preferred_element_type=f32
                )
                value = jnp.maximum(value, 0.0).astype(bf)
                hidden[:, pl.ds(pl.multiple_of(side * depth + at, TILE), TILE)] = value
            return carry

        lax.fori_loop(0, depth // TILE, up, 0)

        def down(n, carry):
            at = pl.ds(pl.multiple_of(n * TILE, TILE), TILE)
            value = jnp.dot(
                hidden[:, :depth], w_second[0, :, at], preferred_element_type=f32
            ) + jnp.dot(hidden[:, depth:], w_second[1, :, at], preferred_element_type=f32)
            result[:, at] = value.astype(bf)
            return carry

        lax.fori_loop(0, width // TILE, down, 0)
        shape = (groups, 4, 5, 16, 128)
        tiles = result[...].reshape(2 * count, 16, 128)
        mate_part[part] = tiles[count:].reshape(shape)
        remote(mate_part.at[part], part_in.at[part], p_send, p_recv.at[c], mate_id).start()
        summed[part] = tiles[:count].reshape(shape)

    def reply(c):
        part = pl.ds(c * groups, groups)
        await_bytes(part_in.at[part], p_recv.at[c])
        total = summed[part].astype(f32) + part_in[part].astype(f32)
        summed[part] = total.astype(bf)

        def send_back(n, carry):
            g = c * groups + n
            for q in (2, 3, 1, 0):
                to = device(4 - g // 4, 4 - g % 4, origin(q))
                copy = remote(summed.at[g, q], back.at[mine], r_send, r_recv.at[g // 4], to)
                if q == 0:

                    @pl.when(g > 0)
                    def _():
                        copy.start()

                    @pl.when(g == 0)
                    def _():
                        pltpu.make_async_copy(
                            summed.at[0, 0], back.at[mine], r_recv.at[0]
                        ).start()

                else:
                    copy.start()
            return carry

        lax.fori_loop(0, groups, send_back, 0)

    def turn(t, carry):
        gather("turn", t)
        pl.when(t < CHUNKS)(lambda: arrive(t))
        gather("arrived", t)

        @pl.when(t == 1)
        def _():
            own_first.wait()
            own_second.wait()
            w1_copy.wait()
            w2_copy.wait()

        pl.when((t >= 1) & (t <= CHUNKS))(lambda: compute(t - 1))
        gather("computed", t)
        pl.when(t >= 2)(lambda: reply(t - 2))
        gather("replied", t)
        return carry

    lax.fori_loop(0, CHUNKS + 2, turn, 0)
    gather("end")

    own_target.wait()
    sentence_copy.wait()
    await_bytes(gathered.at[1 - s], x_recv)

    def weight_tile(at):
        return gathered[:, :, :, :, :, pl.ds(pl.multiple_of(at, TILE), TILE)].reshape(width, TILE)

    def query(n, carry):
        value = jnp.dot(targets[...], weight_tile(n * TILE), preferred_element_type=f32)
        queries[:, pl.ds(pl.multiple_of(n * TILE, TILE), TILE)] = value.astype(bf)
        return carry

    lax.fori_loop(0, 1024 // TILE, query, 0)
    target_rows = targets.shape[0]
    ids = jnp.broadcast_to(target_sentence[...].astype(f32), (128, target_rows)).T
    same = ids == sentence_in[...].astype(f32)

    for dy in range(4):
        block = (y + dy) % 4
        part = pl.ds(block * 16, 16)
        await_bytes(back.at[part], r_recv.at[dy])
        straight[...] = back[part].reshape(80, 16, 128).reshape(80, width)

        def mix(n, carry):
            at = pl.ds(pl.multiple_of(n * TILE, TILE), TILE)
            value = jnp.dot(mixing[0, block], straight[:, at], preferred_element_type=f32)
            value += jnp.dot(mixing[1, block], straight[:, at], preferred_element_type=f32)
            before = source[:, at].astype(f32) if dy == 0 else updated[:, at]
            updated[:, at] = before + value
            return carry

        lax.fori_loop(0, width // TILE, mix, 0)
    memory[...] = (layer_norm(updated[...]) * gain[...]).astype(bf)
    pltpu.make_async_copy(memory, memory_out, o_sem.at[4]).start()

    def project(n, carry):
        for side in range(2):
            value = jnp.dot(
                memory[...],
                weight_tile(1024 * (side + 1) + n * TILE),
                preferred_element_type=f32,
            )
            kv[n, side] = value.astype(bf)
        remote(kv.at[n], kv_in.at[n], k_send, k_recv.at[n], partner).start()
        return carry

    lax.fori_loop(0, 4, project, 0)

    def attend(n, carry):
        await_bytes(kv_in.at[n], k_recv.at[n])
        for side in range(TILE // HDIM):
            inner = slice(side * HDIM, (side + 1) * HDIM)
            at = pl.ds(pl.multiple_of(n * TILE + side * HDIM, HDIM), HDIM)
            scores = lax.dot_general(
                queries[:, at],
                kv_in[n, 0, :, inner],
                (((1,), (1,)), ((), ())),
                preferred_element_type=f32,
            ) * (1.0 / HDIM**0.5)
            scores = jnp.where(same, scores, -jnp.inf)
            peak = jnp.max(scores, axis=-1, keepdims=True)
            raised = jnp.exp(scores - peak)
            probs = (raised * (1.0 / jnp.sum(raised, axis=-1, keepdims=True))).astype(bf)
            mixed = jnp.dot(probs, kv_in[n, 1, :, inner], preferred_element_type=f32)
            context[:, at] = mixed.astype(bf)
        done = pl.ds(pl.multiple_of(n * TILE, TILE), TILE)
        pltpu.make_async_copy(context.at[:, done], context_out.at[:, done], o_sem.at[n]).start()
        return carry

    lax.fori_loop(0, 4, attend, 0)
    await_bytes(kv, k_send)
    for n in range(4):
        await_bytes(context.at[:, pl.ds(n * TILE, TILE)], o_sem.at[n])
    await_bytes(memory, o_sem.at[4])
    await_bytes(back.at[pl.ds(0, 63)], r_send)
    await_bytes(back.at[pl.ds(0, 63)], d_send)
    await_bytes(rows_in.at[0], f_send)
    await_bytes(mate_part, p_send)
    gather_done()


def hand_over(memory, context, memory_out, context_out, sem):
    copies = (
        pltpu.make_async_copy(memory, memory_out, sem.at[0]),
        pltpu.make_async_copy(context, context_out, sem.at[1]),
    )
    for copy in copies:
        copy.start()
    for copy in copies:
        copy.wait()


def body(
    source_tokens,
    routes,
    gates,
    source_sentence,
    expert_in,
    expert_out,
    final_gain,
    target_tokens,
    target_sentence,
    query_weight,
    key_weight,
    value_weight,
):
    bf, f32, dma = jnp.bfloat16, jnp.float32, pltpu.SemaphoreType.DMA
    rows, width = source_tokens.shape
    target_rows = target_tokens.shape[0]
    count = 2 * 320 // CHUNKS
    vmem = pl.BlockSpec(memory_space=pltpu.VMEM)
    hbm = pl.BlockSpec(memory_space=pl.ANY)
    results = pl.pallas_call(
        layer_kernel,
        out_shape=(
            jax.ShapeDtypeStruct((rows, width), bf),
            jax.ShapeDtypeStruct((target_rows, 1024), bf),
        ),
        in_specs=[vmem, vmem, vmem, vmem, hbm, hbm, vmem, hbm, vmem, vmem, vmem, vmem],
        out_specs=(hbm, hbm),
        scratch_shapes=[
            pltpu.VMEM((rows, width), bf),
            pltpu.VMEM((target_rows, 1024), bf),
            pltpu.VMEM((rows, width), bf),
            pltpu.VMEM((384, rows), bf),
            pltpu.VMEM((2, 4, rows, 80), bf),
            pltpu.VMEM((64, 5, 16, 128), bf),
            pltpu.VMEM((2, 16, 4, 5, 16, 128), bf),
            pltpu.VMEM((count, width), bf),
            pltpu.VMEM((2, width, 1024), bf),
            pltpu.VMEM((2, 1024, width), bf),
            pltpu.VMEM((count, width), bf),
            pltpu.VMEM((count, width), bf),
            pltpu.VMEM((16, 4, 5, 16, 128), bf),
            pltpu.VMEM((16, 4, 5, 16, 128), bf),
            pltpu.VMEM((16, 4, 5, 16, 128), bf),
            pltpu.VMEM((8, 3072), f32),
            pltpu.VMEM((8, 3072), f32),
            pltpu.VMEM((2, 4, 4, 4, 16, 3072), bf),
            pltpu.VMEM((64, 5, 16, 128), bf),
            pltpu.VMEM((80, width), bf),
            pltpu.VMEM((rows, width), f32),
            pltpu.VMEM((target_rows, width), bf),
            pltpu.VMEM((target_rows, 1024), bf),
            pltpu.VMEM((4, 2, rows, TILE), bf),
            pltpu.VMEM((4, 2, rows, TILE), bf),
            pltpu.VMEM((1, rows), jnp.int32),
            dma,
            dma((16,)),
            dma,
            dma((CHUNKS,)),
            dma((2,)),
            dma((2,)),
            dma((3,)),
            dma,
            dma((CHUNKS,)),
            dma,
            dma((4,)),
            dma((20,)),
            dma((20,)),
            dma,
            dma,
            dma,
            dma((4,)),
            dma((2,)),
            dma((5,)),
        ],
        compiler_params=pltpu.CompilerParams(
            collective_id=0, has_side_effects=True, vmem_limit_bytes=58 << 20
        ),
        cost_estimate=pl.CostEstimate(
            flops=13 * 10**9, bytes_accessed=20 * 10**6, transcendentals=0
        ),
    )(
        source_tokens,
        routes.T,
        gates.T,
        source_sentence,
        expert_in,
        expert_out,
        final_gain.reshape(1, width),
        target_tokens,
        target_sentence,
        query_weight,
        key_weight,
        value_weight,
    )
    return pl.pallas_call(
        hand_over,
        out_shape=tuple(jax.ShapeDtypeStruct(part.shape, part.dtype) for part in results),
        in_specs=[vmem, vmem],
        out_specs=(hbm, hbm),
        scratch_shapes=[dma((2,))],
    )(*results)


def solution(mesh):
    rows = P(("section", "expert"), None)
    placed = (
        rows,
        rows,
        rows,
        rows,
        P("expert", None, "section"),
        P("expert", "section", None),
        P(),
        rows,
        rows,
        rows,
        rows,
        rows,
    )
    return jax.shard_map(
        body, mesh=mesh, in_specs=placed, out_specs=(rows, rows), check_vma=False
    )
```

```python
import jax
import jax.numpy as jnp
from jax import lax
from jax.experimental import pallas as pl
from jax.experimental.pallas import tpu as pltpu
from jax.sharding import PartitionSpec as P

HDIM = 128
MESH = pl.DeviceIdType.MESH
CHUNKS = 4
TILE = 256
PLAN = {"norm": ((0, 0),), "route": ((0, 1),), "first": ((0, 2),), "arrived": ((0, 3), (1, 4)), "computed": ((1, 5), (3, 6), (4, 7))}


def layer_norm(values):
    mean = jnp.mean(values, axis=-1, keepdims=True)
    centred = values - mean
    spread = jnp.mean(centred * centred, axis=-1, keepdims=True)
    return centred * lax.rsqrt(spread + 1e-05)


def await_bytes(ref, sem):
    pltpu.make_async_copy(ref, ref, sem).wait()


def layer_kernel(
    source,
    routes,
    gates,
    sentence,
    first,
    second,
    gain,
    target,
    target_sentence,
    wq,
    wk,
    wv,
    memory_out,
    context_out,
    memory,
    context,
    normed,
    picked,
    mixing,
    packed,
    rows_in,
    rows,
    w_first,
    w_second,
    hidden,
    result,
    mate_part,
    part_in,
    summed,
    share,
    share_in,
    gathered,
    back,
    straight,
    updated,
    targets,
    queries,
    kv,
    kv_in,
    sentence_in,
    d_send,
    d_recv,
    f_send,
    f_recv,
    w_send,
    w_recv,
    w_local,
    p_send,
    p_recv,
    r_send,
    r_recv,
    a_send,
    a_recv,
    x_send,
    x_recv,
    k_send,
    k_recv,
    s_sem,
    o_sem,
):
    f32, bf = jnp.float32, jnp.bfloat16
    s = lax.axis_index("section")
    j = lax.axis_index("expert")
    y, x, z = j // 32, (j // 8) % 4, j % 8
    k = z // 2
    out = 2 * (z % 2) - 1
    mate = z - out
    mine = (y * 4 + x) * 4 + k

    def device(dy, dx, new_z):
        return (s, (((y + dy) % 4) * 4 + (x + dx) % 4) * 8 + new_z)

    def near(q):
        return (z + (0, out, -2 * out, 3 * out)[q] + 8) % 8

    def origin(q):
        return (z + out * q + 8) % 8

    partner = (1 - s, j)
    mate_id = device(0, 0, mate)
    next_id = device(0, 0, origin(1))

    own_first = pltpu.make_async_copy(first.at[0], w_first.at[0], w_local.at[0])
    own_second = pltpu.make_async_copy(second.at[0], w_second.at[0], w_local.at[1])
    own_target = pltpu.make_async_copy(target, targets, w_local.at[2])
    own_first.start()
    own_second.start()
    own_target.start()

    barrier = pltpu.get_barrier_semaphore()
    spread = (0, 1, 2, -2, 3)

    def greet(dy, dx, step):
        pl.semaphore_signal(
            barrier, inc=1, device_id=device(dy, dx, (z + out * step + 8) % 8), device_id_type=MESH
        )

    def greet_column(g, carry):
        for step in spread:
            greet(g // 4, g % 4, step)
        return carry

    lax.fori_loop(1, 16, greet_column, 0)
    for step in spread[1:]:
        greet(0, 0, step)
    pl.semaphore_signal(barrier, inc=1, device_id=mate_id, device_id_type=MESH)
    pl.semaphore_signal(barrier, inc=1, device_id=partner, device_id_type=MESH)
    for n, part in enumerate((wq, wk, wv)):
        share[:, n * 1024 : (n + 1) * 1024] = part[...].astype(f32)
    count_t, width = source.shape
    normed[...] = layer_norm(source[...].astype(f32)).astype(bf)
    token = lax.broadcasted_iota(jnp.int32, (128, count_t), 1)
    expert = lax.broadcasted_iota(jnp.int32, (128, count_t), 0)
    pick_0 = (routes[0:1, :] == expert).astype(f32)
    pick_1 = (routes[1:2, :] == expert).astype(f32)
    picks = pick_0 + pick_1
    earlier = (expert < token).astype(bf)
    before = jnp.dot(picks.astype(bf), earlier, preferred_element_type=f32)
    slot = lax.broadcasted_iota(jnp.int32, (picked.shape[0], 128), 0)
    owner = lax.broadcasted_iota(jnp.int32, (picked.shape[0], 128), 1)
    wide = ((slot >= owner * 5) & (slot < owner * 5 + 5)).astype(bf)

    def widen(value):
        return jnp.dot(wide, value.astype(bf), preferred_element_type=f32)

    slot_f = slot.astype(f32)
    place = slot_f - 5.0 * jnp.floor((slot_f + 0.5) * 0.2)
    hits = widen(picks) * (widen(before) == place).astype(f32)
    picked[...] = hits.astype(bf)
    weight = pick_0 * gates[0:1, :] + pick_1 * gates[1:2, :]
    weight_high = weight.astype(bf).astype(f32)
    for n, part in enumerate((weight_high, weight - weight_high)):
        mixed = (hits * widen(part)).T.astype(bf)
        for block in range(4):
            mixing[n, block] = mixed[:, block * 80 : (block + 1) * 80]

    pl.semaphore_wait(barrier, 81)

    def remote(src, dst, send, recv, to):
        return pltpu.make_async_remote_copy(
            src_ref=src, dst_ref=dst, send_sem=send, recv_sem=recv, device_id=to, device_id_type=MESH
        )

    share_copy = remote(share, share_in, a_send.at[0], a_recv.at[0], mate_id)
    share_copy.start()
    sentence_copy = remote(sentence, sentence_in, s_sem.at[0], s_sem.at[1], partner)
    sentence_copy.start()
    w1_copy = remote(first.at[0], w_first.at[1], w_send.at[0], w_recv.at[0], partner)
    w2_copy = remote(second.at[0], w_second.at[1], w_send.at[1], w_recv.at[1], partner)
    w1_copy.start()
    w2_copy.start()

    here = gathered.at[s, y, x]
    plus, minus = (k + out + 4) % 4, (k - out + 4) % 4
    half = gathered.shape[5] // 2
    cols = (pl.ds(0, half), pl.ds(half, half))
    xl, xr = (x + 3) % 4, (x + 1) % 4
    yl, yr = (y + 3) % 4, (y + 1) % 4
    x2, y2 = (x + 2) % 4, (y + 2) % 4
    id_xl, id_xr = device(0, 3, z), device(0, 1, z)
    id_yl, id_yr = device(3, 0, z), device(1, 0, z)
    every, lo, hi = pl.ds(0, 4), pl.ds(0, 2), pl.ds(2, 2)

    def along(ref, n, to):
        remote(ref, ref, a_send.at[n], a_recv.at[n], to).start()

    def across(ref):
        remote(ref, ref, x_send, x_recv, partner).start()

    def block_a(yy, xx, ks=every):
        return gathered.at[s, yy, xx, ks, :, cols[0]]

    def block_b(yy, xx, ks=every):
        return gathered.at[s, yy, xx, ks, :, cols[1]]

    def row_a(yy, ks=every):
        return gathered.at[s, yy, :, ks, :, cols[0]]

    def row_b(xx, ks=every):
        return gathered.at[s, :, xx, ks, :, cols[1]]

    def gather_0():
        share_copy.wait()
        low = jnp.where(z % 2 == 0, share[...], share_in[...])
        high = jnp.where(z % 2 == 0, share_in[...], share[...])
        gathered[s, y, x, k] = jnp.concatenate([low, high], axis=0).astype(bf)
        along(here.at[k], 1, next_id)

    def gather_1():
        await_bytes(here.at[plus], a_recv.at[1])
        along(here.at[plus], 2, mate_id)

    def gather_2():
        await_bytes(here.at[minus], a_recv.at[2])
        along(here.at[minus], 3, next_id)

    def gather_3():
        await_bytes(here.at[(k + 2) % 4], a_recv.at[3])
        along(block_a(y, x), 4, id_xr)
        along(block_b(y, x), 6, id_yr)
        along(block_a(y, x), 5, id_xl)
        along(block_b(y, x), 7, id_yl)
        across(here)

    def gather_4():
        await_bytes(block_a(y, xl), a_recv.at[4])
        along(block_a(y, xl, lo), 8, id_xr)
        await_bytes(block_b(yl, x), a_recv.at[6])
        along(block_b(yl, x, lo), 10, id_yr)
        await_bytes(block_a(y, xr), a_recv.at[5])
        along(block_a(y, xr, hi), 9, id_xl)
        await_bytes(block_b(yr, x), a_recv.at[7])
        along(block_b(yr, x, hi), 11, id_yl)
        for ref in (block_a(y, xl), block_b(yl, x), block_a(y, xr), block_b(yr, x)):
            across(ref)

    def gather_5():
        await_bytes(block_a(y, x2, lo), a_recv.at[8])
        await_bytes(block_a(y, x2, hi), a_recv.at[9])
        along(row_a(y), 12, id_yr)
        along(row_a(y), 13, id_yl)
        await_bytes(block_b(y2, x, lo), a_recv.at[10])
        await_bytes(block_b(y2, x, hi), a_recv.at[11])
        along(row_b(x), 14, id_xr)
        along(row_b(x), 15, id_xl)
        across(block_a(y, x2))
        across(block_b(y2, x))

    def gather_6():
        await_bytes(row_a(yl), a_recv.at[12])
        along(row_a(yl, lo), 16, id_yr)
        await_bytes(row_b(xl), a_recv.at[14])
        along(row_b(xl, lo), 18, id_xr)
        await_bytes(row_a(yr), a_recv.at[13])
        along(row_a(yr, hi), 17, id_yl)
        await_bytes(row_b(xr), a_recv.at[15])
        along(row_b(xr, hi), 19, id_xl)
        for ref in (row_a(yl), row_b(xl), row_a(yr), row_b(xr)):
            across(ref)

    def gather_7():
        await_bytes(row_a(y2, lo), a_recv.at[16])
        await_bytes(row_a(y2, hi), a_recv.at[17])
        across(row_a(y2))
        await_bytes(row_b(x2, lo), a_recv.at[18])
        await_bytes(row_b(x2, hi), a_recv.at[19])
        across(row_b(x2))

    def gather_done():
        for n in (1, 2, 3):
            await_bytes(here.at[k], a_send.at[n])
        for n in range(4, 8):
            await_bytes(block_a(y, x), a_send.at[n])
        for n in range(8, 12):
            await_bytes(block_a(y, x, lo), a_send.at[n])
        for n in range(12, 16):
            await_bytes(row_a(y), a_send.at[n])
        for n in range(16, 20):
            await_bytes(row_a(y, lo), a_send.at[n])
        await_bytes(gathered.at[s], x_send)

    steps = (gather_0, gather_1, gather_2, gather_3, gather_4, gather_5, gather_6, gather_7)

    def gather(place, t=None):
        for when, step in PLAN.get(place, ()):
            if t is None:
                steps[step]()
            else:
                pl.when(t == when)(steps[step])

    gather("norm")
    gather("route")

    kept = pltpu.make_async_copy(packed.at[mine], rows_in.at[0, 0, 0], d_recv.at[0])

    def send_one(dy, dx, q):
        g = dy * 4 + dx
        goal = near(q)
        expert = (((y + dy) % 4) * 4 + (x + dx) % 4) * 4 + goal // 2
        remote(
            packed.at[expert], rows_in.at[0, g, q], d_send, d_recv.at[g], device(dy, dx, goal)
        ).start()

    for dy in range(4):
        block = (y + dy) % 4
        chosen = picked[pl.ds(pl.multiple_of(block * 80, 16), 80), :]
        rows80 = jnp.dot(chosen, normed[...], preferred_element_type=f32).astype(bf)
        packed[pl.ds(block * 16, 16)] = rows80.reshape(80, 16, 128).reshape(16, 5, 16, 128)
        if dy == 0:
            kept.start()
            for q in (3, 2, 1):
                send_one(0, 0, q)

        def send_dx(dx, carry):
            for q in (3, 2, 1, 0):
                send_one(dy, dx, q)
            return carry

        lax.fori_loop(1 if dy == 0 else 0, 4, send_dx, 0)
        if dy == 0:
            gather("first")
    gather("sent")

    groups = 16 // CHUNKS
    count = groups * 4 * 5

    def arrive(c):
        def one(n, carry):
            g = c * groups + n
            await_bytes(rows_in.at[0, g], d_recv.at[g])
            remote(rows_in.at[0, g], rows_in.at[1, g], f_send, f_recv.at[c], mate_id).start()
            return carry

        lax.fori_loop(0, groups, one, 0)

    def compute(c):
        part = pl.ds(c * groups, groups)
        await_bytes(rows_in.at[1, part], f_recv.at[c])
        tiles = rows_in[:, part].reshape(2 * count, 16, 128)
        rows[...] = tiles.reshape(2 * count, width)
        depth = w_first.shape[2]

        def up(n, carry):
            for side in range(2):
                at = pl.multiple_of(n * TILE, TILE)
                value = jnp.dot(
                    rows[...], w_first[side, :, pl.ds(at, TILE)], preferred_element_type=f32
                )
                value = jnp.maximum(value, 0.0).astype(bf)
                hidden[:, pl.ds(pl.multiple_of(side * depth + at, TILE), TILE)] = value
            return carry

        lax.fori_loop(0, depth // TILE, up, 0)

        def down(n, carry):
            at = pl.ds(pl.multiple_of(n * TILE, TILE), TILE)
            value = jnp.dot(
                hidden[:, :depth], w_second[0, :, at], preferred_element_type=f32
            ) + jnp.dot(hidden[:, depth:], w_second[1, :, at], preferred_element_type=f32)
            result[:, at] = value.astype(bf)
            return carry

        lax.fori_loop(0, width // TILE, down, 0)
        shape = (groups, 4, 5, 16, 128)
        tiles = result[...].reshape(2 * count, 16, 128)
        mate_part[part] = tiles[count:].reshape(shape)
        remote(mate_part.at[part], part_in.at[part], p_send, p_recv.at[c], mate_id).start()
        summed[part] = tiles[:count].reshape(shape)

    def reply(c):
        part = pl.ds(c * groups, groups)
        await_bytes(part_in.at[part], p_recv.at[c])
        total = summed[part].astype(f32) + part_in[part].astype(f32)
        summed[part] = total.astype(bf)

        def send_back(n, carry):
            g = c * groups + n
            for q in (3, 2, 1, 0):
                to = device(4 - g // 4, 4 - g % 4, origin(q))
                copy = remote(summed.at[g, q], back.at[mine], r_send, r_recv.at[g // 4], to)
                if q == 0:

                    @pl.when(g > 0)
                    def _():
                        copy.start()

                    @pl.when(g == 0)
                    def _():
                        pltpu.make_async_copy(
                            summed.at[0, 0], back.at[mine], r_recv.at[0]
                        ).start()

                else:
                    copy.start()
            return carry

        lax.fori_loop(0, groups, send_back, 0)

    def turn(t, carry):
        gather("turn", t)
        pl.when(t < CHUNKS)(lambda: arrive(t))
        gather("arrived", t)

        @pl.when(t == 1)
        def _():
            own_first.wait()
            own_second.wait()
            w1_copy.wait()
            w2_copy.wait()

        pl.when((t >= 1) & (t <= CHUNKS))(lambda: compute(t - 1))
        gather("computed", t)
        pl.when(t >= 2)(lambda: reply(t - 2))
        gather("replied", t)
        return carry

    lax.fori_loop(0, CHUNKS + 2, turn, 0)
    gather("end")

    own_target.wait()
    sentence_copy.wait()
    await_bytes(gathered.at[1 - s], x_recv)

    def weight_tile(at):
        return gathered[:, :, :, :, :, pl.ds(pl.multiple_of(at, TILE), TILE)].reshape(width, TILE)

    def query(n, carry):
        value = jnp.dot(targets[...], weight_tile(n * TILE), preferred_element_type=f32)
        queries[:, pl.ds(pl.multiple_of(n * TILE, TILE), TILE)] = value.astype(bf)
        return carry

    lax.fori_loop(0, 1024 // TILE, query, 0)
    target_rows = targets.shape[0]
    ids = jnp.broadcast_to(target_sentence[...].astype(f32), (128, target_rows)).T
    same = ids == sentence_in[...].astype(f32)

    for dy in range(4):
        block = (y + dy) % 4
        part = pl.ds(block * 16, 16)
        await_bytes(back.at[part], r_recv.at[dy])
        straight[...] = back[part].reshape(80, 16, 128).reshape(80, width)

        def mix(n, carry):
            at = pl.ds(pl.multiple_of(n * TILE, TILE), TILE)
            value = jnp.dot(mixing[0, block], straight[:, at], preferred_element_type=f32)
            value += jnp.dot(mixing[1, block], straight[:, at], preferred_element_type=f32)
            before = source[:, at].astype(f32) if dy == 0 else updated[:, at]
            updated[:, at] = before + value
            return carry

        lax.fori_loop(0, width // TILE, mix, 0)
    memory[...] = (layer_norm(updated[...]) * gain[...]).astype(bf)
    pltpu.make_async_copy(memory, memory_out, o_sem.at[4]).start()

    def project(n, carry):
        for side in range(2):
            value = jnp.dot(
                memory[...],
                weight_tile(1024 * (side + 1) + n * TILE),
                preferred_element_type=f32,
            )
            kv[n, side] = value.astype(bf)
        remote(kv.at[n], kv_in.at[n], k_send, k_recv.at[n], partner).start()
        return carry

    lax.fori_loop(0, 4, project, 0)

    def attend(n, carry):
        await_bytes(kv_in.at[n], k_recv.at[n])
        for side in range(TILE // HDIM):
            inner = slice(side * HDIM, (side + 1) * HDIM)
            at = pl.ds(pl.multiple_of(n * TILE + side * HDIM, HDIM), HDIM)
            scores = lax.dot_general(
                queries[:, at],
                kv_in[n, 0, :, inner],
                (((1,), (1,)), ((), ())),
                preferred_element_type=f32,
            ) * (1.0 / HDIM**0.5)
            scores = jnp.where(same, scores, -jnp.inf)
            peak = jnp.max(scores, axis=-1, keepdims=True)
            raised = jnp.exp(scores - peak)
            probs = (raised * (1.0 / jnp.sum(raised, axis=-1, keepdims=True))).astype(bf)
            mixed = jnp.dot(probs, kv_in[n, 1, :, inner], preferred_element_type=f32)
            context[:, at] = mixed.astype(bf)
        done = pl.ds(pl.multiple_of(n * TILE, TILE), TILE)
        pltpu.make_async_copy(context.at[:, done], context_out.at[:, done], o_sem.at[n]).start()
        return carry

    lax.fori_loop(0, 4, attend, 0)
    await_bytes(kv, k_send)
    for n in range(4):
        await_bytes(context.at[:, pl.ds(n * TILE, TILE)], o_sem.at[n])
    await_bytes(memory, o_sem.at[4])
    await_bytes(back.at[pl.ds(0, 63)], r_send)
    await_bytes(back.at[pl.ds(0, 63)], d_send)
    await_bytes(rows_in.at[0], f_send)
    await_bytes(mate_part, p_send)
    gather_done()


def hand_over(memory, context, memory_out, context_out, sem):
    copies = (
        pltpu.make_async_copy(memory, memory_out, sem.at[0]),
        pltpu.make_async_copy(context, context_out, sem.at[1]),
    )
    for copy in copies:
        copy.start()
    for copy in copies:
        copy.wait()


def body(
    source_tokens,
    routes,
    gates,
    source_sentence,
    expert_in,
    expert_out,
    final_gain,
    target_tokens,
    target_sentence,
    query_weight,
    key_weight,
    value_weight,
):
    bf, f32, dma = jnp.bfloat16, jnp.float32, pltpu.SemaphoreType.DMA
    rows, width = source_tokens.shape
    target_rows = target_tokens.shape[0]
    count = 2 * 320 // CHUNKS
    vmem = pl.BlockSpec(memory_space=pltpu.VMEM)
    hbm = pl.BlockSpec(memory_space=pl.ANY)
    results = pl.pallas_call(
        layer_kernel,
        out_shape=(
            jax.ShapeDtypeStruct((rows, width), bf),
            jax.ShapeDtypeStruct((target_rows, 1024), bf),
        ),
        in_specs=[vmem, vmem, vmem, vmem, hbm, hbm, vmem, hbm, vmem, vmem, vmem, vmem],
        out_specs=(hbm, hbm),
        scratch_shapes=[
            pltpu.VMEM((rows, width), bf),
            pltpu.VMEM((target_rows, 1024), bf),
            pltpu.VMEM((rows, width), bf),
            pltpu.VMEM((384, rows), bf),
            pltpu.VMEM((2, 4, rows, 80), bf),
            pltpu.VMEM((64, 5, 16, 128), bf),
            pltpu.VMEM((2, 16, 4, 5, 16, 128), bf),
            pltpu.VMEM((count, width), bf),
            pltpu.VMEM((2, width, 1024), bf),
            pltpu.VMEM((2, 1024, width), bf),
            pltpu.VMEM((count, width), bf),
            pltpu.VMEM((count, width), bf),
            pltpu.VMEM((16, 4, 5, 16, 128), bf),
            pltpu.VMEM((16, 4, 5, 16, 128), bf),
            pltpu.VMEM((16, 4, 5, 16, 128), bf),
            pltpu.VMEM((8, 3072), f32),
            pltpu.VMEM((8, 3072), f32),
            pltpu.VMEM((2, 4, 4, 4, 16, 3072), bf),
            pltpu.VMEM((64, 5, 16, 128), bf),
            pltpu.VMEM((80, width), bf),
            pltpu.VMEM((rows, width), f32),
            pltpu.VMEM((target_rows, width), bf),
            pltpu.VMEM((target_rows, 1024), bf),
            pltpu.VMEM((4, 2, rows, TILE), bf),
            pltpu.VMEM((4, 2, rows, TILE), bf),
            pltpu.VMEM((1, rows), jnp.int32),
            dma,
            dma((16,)),
            dma,
            dma((CHUNKS,)),
            dma((2,)),
            dma((2,)),
            dma((3,)),
            dma,
            dma((CHUNKS,)),
            dma,
            dma((4,)),
            dma((20,)),
            dma((20,)),
            dma,
            dma,
            dma,
            dma((4,)),
            dma((2,)),
            dma((5,)),
        ],
        compiler_params=pltpu.CompilerParams(
            collective_id=0, has_side_effects=True, vmem_limit_bytes=58 << 20
        ),
        cost_estimate=pl.CostEstimate(
            flops=13 * 10**9, bytes_accessed=20 * 10**6, transcendentals=0
        ),
    )(
        source_tokens,
        routes.T,
        gates.T,
        source_sentence,
        expert_in,
        expert_out,
        final_gain.reshape(1, width),
        target_tokens,
        target_sentence,
        query_weight,
        key_weight,
        value_weight,
    )
    return pl.pallas_call(
        hand_over,
        out_shape=tuple(jax.ShapeDtypeStruct(part.shape, part.dtype) for part in results),
        in_specs=[vmem, vmem],
        out_specs=(hbm, hbm),
        scratch_shapes=[dma((2,))],
    )(*results)


def solution(mesh):
    rows = P(("section", "expert"), None)
    placed = (
        rows,
        rows,
        rows,
        rows,
        P("expert", None, "section"),
        P("expert", "section", None),
        P(),
        rows,
        rows,
        rows,
        rows,
        rows,
    )
    return jax.shard_map(
        body, mesh=mesh, in_specs=placed, out_specs=(rows, rows), check_vma=False
    )
```
